512 devices in a mesh: ctx: 64 (over z, x), head: 8 (over y, core).
Axes of the slice: x: 4, y: 4, z: 16, core: 2. Of those that a mesh axis runs over, the one named last changes fastest.
Arguments:
- queries: bfloat16 [16384, 32, 576], P('ctx', 'head'), may hold values from -1024 to 1024
- latent_kv: bfloat16 [16384, 576], P('ctx'), may hold values from -6 to 6
- out_grad: bfloat16 [16384, 32, 512], P('ctx', 'head'), may hold values from -6 to 6
- lengths: int32 [32], replicated, may hold values from 1 to 1024, as said below
- block_plan: int32 [128], replicated, may hold values from 0 to 63, as said below
Outputs:
- query_grad: bfloat16 [16384, 32, 576], P('ctx', 'head')
- latent_grad: float32 [16384, 576], P(('ctx', 'head'))
The draws below stay inside these ranges and needn't reach their ends.
Inputs may be any that keep to these rules, and one draw needn't show every extreme that they name: `lengths`: 32 documents laid end to end; they sum to 16384, and one has exactly 1024 tokens. `block_plan`: block b is held by device b // 2, except that the last block of a device may trade places with the last block of the device 64 // 2 indices away on ctx; trades are mutual, and the last device on ctx always trades.
All inputs are finite; a program needn't handle non-finite values.
Results may differ from the reference program's by a relative error of at most 0.0049.
Values may be sent and summed in bfloat16 or wider, within the bound.
A program may use at most 128 MiB of HBM per device.

```python
import jax
import jax.numpy as jnp
from jax import lax

HEADS = 32
LATENT = 512
ROPE = 64
BLOCK = 128
MOST = 1024
QK = 576
TOKENS = 16384
BLK_DEV = 2
BLOCKS = 128
DOCS = 32
N_CTX = 64


def layout_draw(key):
    jitter_key, long_key = jax.random.split(key)
    remaining = TOKENS - MOST
    others_count = DOCS - 1
    base_len = remaining // others_count
    leftover = remaining % others_count
    jitter = jax.random.randint(jitter_key, (others_count,), 0, base_len // 2 + 1)
    others = base_len + (jnp.arange(others_count) < leftover).astype(jnp.int32) + jitter - jnp.roll(jitter, -1)
    long_slot = jax.random.randint(long_key, (), 0, DOCS)
    doc_slot = jnp.arange(DOCS, dtype=jnp.int32)
    shifted = jnp.clip(jnp.where(doc_slot > long_slot, doc_slot - 1, doc_slot), 0, others_count - 1)
    lengths = jnp.where(doc_slot == long_slot, MOST, others[shifted]).astype(jnp.int32)
    doc_ends = jnp.cumsum(lengths)
    doc_starts = doc_ends - lengths
    block_first = jnp.arange(BLOCKS, dtype=jnp.int32) * BLOCK
    owner = jnp.sum((doc_ends[None, :] <= block_first[:, None]).astype(jnp.int32), axis=1)
    tile_load = jnp.arange(BLOCKS, dtype=jnp.int32) - doc_starts[owner] // BLOCK + 1
    grouped = tile_load.reshape(N_CTX, BLK_DEV)
    device_load = jnp.sum(grouped, axis=1)
    last_load = grouped[:, BLK_DEV - 1]
    half_axis = N_CTX // 2
    lower_load, upper_load = (device_load[:half_axis], device_load[half_axis:])
    lower_last, upper_last = (last_load[:half_axis], last_load[half_axis:])
    before = jnp.maximum(lower_load, upper_load)
    after = jnp.maximum(lower_load - lower_last + upper_last, upper_load - upper_last + lower_last)
    forced = jnp.arange(half_axis, dtype=jnp.int32) == half_axis - 1
    pair_trade = (after < before) | forced
    do_trade = jnp.concatenate([pair_trade, pair_trade])
    device_ids = jnp.arange(N_CTX, dtype=jnp.int32)
    partner = (device_ids + half_axis) % N_CTX
    last_dest = jnp.where(do_trade, partner, device_ids)
    holders = jnp.repeat(device_ids, BLK_DEV).reshape(N_CTX, BLK_DEV)
    holders = holders.at[:, BLK_DEV - 1].set(last_dest)
    return (lengths, holders.reshape(BLOCKS).astype(jnp.int32))


def latent_rows(key):
    base_key, fresh_key = jax.random.split(key)
    base_rows = jax.random.truncated_normal(base_key, -6.0, 6.0, (TOKENS, QK), jnp.float32)
    fresh_rope = jax.random.truncated_normal(fresh_key, -6.0, 6.0, (TOKENS, ROPE), jnp.float32)
    picked = (jnp.arange(TOKENS) % 16 == 13)[:, None]
    rope_rows = jnp.clip(jnp.where(picked, fresh_rope, base_rows[:, LATENT:]), -6.0, 6.0)
    return jnp.concatenate([base_rows[:, :LATENT], rope_rows], axis=1)


def draw_lengths(key, part):
    lengths, block_plan = layout_draw(key)
    return lengths


def draw_block_plan(key, part):
    lengths, block_plan = layout_draw(key)
    return block_plan


def draw_latent_kv(key, part):
    shared = latent_rows(key)
    return shared.astype(jnp.bfloat16)


def draw_queries(key, part):
    key = jax.random.fold_in(key, 11)
    return jax.random.truncated_normal(key, -6.0, 6.0, (TOKENS, HEADS, QK), jnp.float32).astype(jnp.bfloat16)


def shard_levels(key, dims, shards, smallest, largest):
    level = 1.0
    for dim, blocks in shards:
        draws = jax.random.uniform(jax.random.fold_in(jax.random.fold_in(key, 6), dim), (blocks,), jnp.float32, smallest / len(shards), largest / len(shards))
        level = level * jnp.repeat(jnp.exp(draws), dims[dim] // blocks).reshape((-1,) + (1,) * (len(dims) - 1 - dim))
    return level


def gaussian(key, dims, spread, reach, shards=(), held_as=jnp.bfloat16):
    gain = shard_levels(key, dims, shards, -0.22, 0.18) if shards else 1.0
    result = jax.random.normal(key, dims, jnp.float32) * spread * gain
    return jnp.minimum(jnp.maximum(result, -reach), reach).astype(held_as)


def setup_inputs(seed: int = 0) -> dict:
    streams_of = jax.random.split(jax.random.key(seed), 6)
    return {
        "queries": draw_queries(jax.random.fold_in(streams_of[5], 71), 0),
        "latent_kv": draw_latent_kv(jax.random.fold_in(streams_of[5], 71), 0),
        "out_grad": gaussian(streams_of[2], (TOKENS, HEADS, LATENT), 1.0, 6.0, ((0, 64), (1, 8))),
        "lengths": draw_lengths(jax.random.fold_in(streams_of[5], 71), 0),
        "block_plan": draw_block_plan(jax.random.fold_in(streams_of[5], 71), 0),
    }


SCORE_SCALE = 192.0 ** -0.5
MASKED_FILL = -1e30


def doc_index(positions, doc_ends):
    inside = jnp.sum((doc_ends[None, :] <= positions[:, None]).astype(jnp.int32), axis=1)
    return jnp.where(positions < 0, -1, inside).astype(jnp.int32)


def reference(queries, latent_kv, out_grad, lengths, block_plan):
    doc_ends = jnp.cumsum(lengths).astype(jnp.int32)
    doc_ids = doc_index(jnp.arange(TOKENS, dtype=jnp.int32), doc_ends)
    padded_keys = jnp.concatenate([jnp.zeros((MOST, QK), jnp.bfloat16), latent_kv], axis=0)
    padded_docs = jnp.concatenate([jnp.full((MOST,), -1, jnp.int32), doc_ids], axis=0)
    span_rows = MOST + BLOCK
    query_blocks = queries.reshape(BLOCKS, BLOCK, HEADS, QK)
    grad_blocks = out_grad.reshape(BLOCKS, BLOCK, HEADS, LATENT)

    def advance(key_grad, inputs):
        block_index, query_block, grad_block = inputs
        row_begin = (block_index * BLOCK).astype(jnp.int32)
        key_rows = lax.dynamic_slice_in_dim(padded_keys, row_begin, span_rows, 0)
        key_docs = lax.dynamic_slice_in_dim(padded_docs, row_begin, span_rows, 0)
        key_pos = row_begin - MOST + jnp.arange(span_rows, dtype=jnp.int32)
        query_pos = row_begin + jnp.arange(BLOCK, dtype=jnp.int32)
        query_docs = lax.dynamic_slice_in_dim(doc_ids, row_begin, BLOCK, 0)
        allowed = (key_docs[None, :] == query_docs[:, None]) & (key_pos[None, :] <= query_pos[:, None])
        query_wide = query_block.astype(jnp.float32)
        key_wide = key_rows.astype(jnp.float32)
        grad_wide = grad_block.astype(jnp.float32)
        scores = jnp.einsum("thc,kc->thk", query_wide, key_wide) * SCORE_SCALE
        scores = jnp.where(allowed[:, None, :], scores, MASKED_FILL)
        row_top = jnp.max(scores, axis=2)
        weights = jnp.exp(scores - row_top[:, :, None])
        row_total = jnp.sum(weights, axis=2)
        probability = weights / row_total[:, :, None]
        values_grad = jnp.einsum("thl,kl->thk", grad_wide, key_wide[:, :LATENT])
        delta = jnp.sum(probability * values_grad, axis=2)
        score_grad = lax.optimization_barrier((probability * (values_grad - delta[:, :, None])).astype(jnp.bfloat16)).astype(jnp.float32)
        probs_low = lax.optimization_barrier(probability.astype(jnp.bfloat16)).astype(jnp.float32)
        query_part = SCORE_SCALE * jnp.einsum("thk,kc->thc", score_grad, key_wide)
        key_part = SCORE_SCALE * jnp.einsum("thk,thc->kc", score_grad, query_wide)
        value_part = jnp.einsum("thk,thl->kl", probs_low, grad_wide)
        tile_grad = key_part + jnp.pad(value_part, ((0, 0), (0, ROPE)))
        current = lax.dynamic_slice_in_dim(key_grad, row_begin, span_rows, 0)
        key_grad = lax.dynamic_update_slice_in_dim(key_grad, current + tile_grad, row_begin, 0)
        return key_grad, query_part.astype(jnp.bfloat16)

    start_grad = jnp.zeros((MOST + TOKENS, QK), jnp.float32)
    key_grad, query_parts = lax.scan(advance, start_grad, (jnp.arange(BLOCKS, dtype=jnp.int32), query_blocks, grad_blocks))
    target = (block_plan * BLK_DEV + jnp.arange(BLOCKS, dtype=jnp.int32) % BLK_DEV).astype(jnp.int32)
    placed = jnp.zeros_like(query_parts).at[target].set(query_parts)
    return placed.reshape(TOKENS, HEADS, QK), key_grad[MOST:]
```

```python
import functools

import jax
import jax.numpy as jnp
from jax import lax
from jax.experimental import pallas as pl
from jax.experimental.pallas import tpu as pltpu
from jax.sharding import PartitionSpec as P

BLOCK = 128
SCORE_SCALE = 192.0 ** (-0.5)
MASKED_FILL = -1e30
MESH = pl.DeviceIdType.MESH

HEADS_DEV = 4
TOK = 256
ROWS = TOK * HEADS_DEV
QK = 576
LAT = 512
WIDE = 640
BACK = 4
WIN = (BACK + 1) * TOK
CHUNK = 256
TILE = 128
PIECE = 32
HALF = TOK // 2

NT = (((1,), (1,)), ((), ()))


def mm(a, b):
    return jnp.dot(a, b, preferred_element_type=jnp.float32)


def mm_nt(a, b):
    return lax.dot_general(a, b, NT, preferred_element_type=jnp.float32)


def fused(
    q_hbm, k_hbm, g_hbm, len_ref,
    dq0_out, own_out, got_out, lat_out,
    q_in, k_in, g_in, q_all, g_all, win, win_t, scores, vgrads, probs, sgrads,
    top, start_of, pos_of, grads, dq0, dq1,
    r1_out, r1_in, r2_out, r2_in, r3_out, r3_in, r4_out, r4_in, lat,
    in_sem, out_sem, s1, v1, s2, v2, s3, v3, st, vt, sr1, vr1, sr2, vr2, sr3, vr3, sr4, vr4,
):
    ctx = lax.axis_index("ctx")
    head = lax.axis_index("head")
    n_ctx = lax.axis_size("ctx")
    n_y = 4
    y = head // 2
    core = head % 2
    x = ctx % 4
    zbase = ctx - x

    def at_ctx(by):
        return {"ctx": lax.rem(ctx + by + n_ctx, n_ctx)}

    def at_y(by):
        return {"head": lax.rem(y + by, n_y) * 2 + core}

    sibling = {"head": y * 2 + (1 - core)}

    peers = [at_ctx(b) for b in (1, 2, 3, 4, -1, -2, -3, -4, n_ctx // 2)]
    peers += [at_y(b) for b in (1, 2, 3)] + [sibling]
    barrier = pltpu.get_barrier_semaphore()
    for peer in peers:
        pl.semaphore_signal(barrier, inc=1, device_id=peer, device_id_type=MESH)

    load_k = pltpu.make_async_copy(k_hbm, k_in, in_sem.at[0])
    load_q = pltpu.make_async_copy(q_hbm, q_in, in_sem.at[1])
    load_g = pltpu.make_async_copy(g_hbm, g_in, in_sem.at[2])
    load_k.start()
    load_q.start()
    load_g.start()
    load_k.wait()

    own0 = BACK * TOK
    keys = jnp.transpose(k_in[...])
    win[pl.ds(own0, TOK), QK:] = jnp.zeros((TOK, WIDE - QK), jnp.bfloat16)
    for c in range(2):
        for yy in range(4):
            at = own0 + c * HALF + yy * PIECE
            frm = yy * 2 * PIECE + c * PIECE
            win[at:at + PIECE, :QK] = keys[frm:frm + PIECE, :]

    mine = core * HALF + y * PIECE
    pl.semaphore_wait(barrier, len(peers))

    def piece(slot):
        return win.at[pl.ds(pl.multiple_of(slot * TOK + mine, PIECE), PIECE), :]

    def half(slot):
        return win.at[pl.ds(pl.multiple_of(slot * TOK + core * HALF, HALF), HALF), :]

    def remote(src, dst, ss, rs, to):
        return pltpu.make_async_remote_copy(
            src_ref=src, dst_ref=dst, send_sem=ss, recv_sem=rs, device_id=to, device_id_type=MESH
        )

    hops = (4, 1, 3, 2)
    first = [remote(piece(BACK), piece(BACK - d), s1.at[d - 1], v1.at[d - 1], at_ctx(d)) for d in hops]
    for copy in first:
        copy.start()

    load_q.wait()
    q_all[QK:, :] = jnp.zeros((WIDE - QK, ROWS), jnp.bfloat16)
    for b in range(2):
        for h in range(HEADS_DEV):
            at = b * 512 + h * BLOCK
            q_all[:QK, at:at + BLOCK] = q_in[h, :, b * BLOCK:(b + 1) * BLOCK]

    lane = lax.broadcasted_iota(jnp.int32, (1, ROWS), 1)
    q_pos = ctx * TOK + (lane // 512) * BLOCK + lane % BLOCK
    begin = jnp.zeros((1, ROWS), jnp.int32)
    total = jnp.int32(0)
    for d in range(len_ref.shape[0]):
        begin = jnp.where(q_pos >= total, total, begin)
        total = total + len_ref[d]
    pos_of[...] = q_pos
    start_of[...] = begin
    top[...] = jnp.full(top.shape, MASKED_FILL, jnp.float32)

    load_g.wait()
    to_row = lax.broadcasted_iota(jnp.int32, (CHUNK, CHUNK), 0)
    from_row = lax.broadcasted_iota(jnp.int32, (CHUNK, CHUNK), 1)
    shuffle = (from_row == (to_row % 64) * HEADS_DEV + to_row // 64).astype(jnp.bfloat16)
    for k in range(4):
        rows = g_in[k * 64:(k + 1) * 64].reshape(CHUNK, LAT)
        rows = mm(shuffle, rows).astype(jnp.bfloat16)
        for h in range(HEADS_DEV):
            at = (k // 2) * 512 + h * BLOCK + (k % 2) * 64
            g_all[at:at + 64, :] = rows[h * 64:(h + 1) * 64, :]

    def tile_scores(slot):
        at = slot * TOK
        keys = win[at:at + TOK, :]
        win_t[:, at:at + TOK] = jnp.transpose(keys)
        row = lax.broadcasted_iota(jnp.int32, (TOK, CHUNK), 0)
        k_pos = (ctx - BACK + slot) * TOK + ((row % HALF) // PIECE) * 2 * PIECE + (row // HALF) * PIECE + row % PIECE

        def chunk(n, _):
            lanes = pl.ds(pl.multiple_of(n * CHUNK, CHUNK), CHUNK)
            s = mm(keys, q_all[:, lanes]) * SCORE_SCALE
            allowed = (k_pos >= start_of[:, lanes]) & (k_pos <= pos_of[:, lanes])
            s = jnp.where(allowed, s, MASKED_FILL)
            scores[at:at + TOK, lanes] = s
            top[:, lanes] = jnp.maximum(top[:, lanes], jnp.max(s.reshape(TOK // 8, 8, CHUNK), axis=0))
            vgrads[at:at + TOK, lanes] = mm_nt(keys[:, :LAT], g_all[lanes, :])
            return 0

        lax.fori_loop(0, ROWS // CHUNK, chunk, 0)

    second = {}
    for i, d in enumerate(hops):
        first[i].wait_recv()
        second[d] = [
            remote(piece(BACK - d), piece(BACK - d), s2.at[d - 1, b - 1], v2.at[d - 1, b - 1], at_y(b)) for b in (1, 3, 2)
        ]
        for copy in second[d]:
            copy.start()

    tile_scores(BACK)
    third = []
    for d in hops:
        for copy in second[d]:
            copy.wait_recv()
        copy = remote(half(BACK - d), half(BACK - d), s3.at[d - 1], v3.at[d - 1], sibling)
        copy.start()
        third.append(copy)
    for i, d in enumerate(hops):
        third[i].wait_recv()
        tile_scores(BACK - d)

    def query_chunk(n, dq):
        lanes = slice(n * CHUNK, (n + 1) * CHUNK)
        peak = jnp.max(top[:, lanes], axis=0, keepdims=True)

        def weigh(i, carry):
            denom, mix = carry
            rows = pl.ds(pl.multiple_of(i * TILE, TILE), TILE)
            p = jnp.exp(scores[rows, lanes] - peak)
            scores[rows, lanes] = p
            pd = p * vgrads[rows, lanes]
            denom = denom + jnp.sum(p.reshape(TILE // 8, 8, CHUNK), axis=0)
            mix = mix + jnp.sum(pd.reshape(TILE // 8, 8, CHUNK), axis=0)
            return denom, mix

        zero = jnp.zeros((8, CHUNK), jnp.float32)
        denom, mix = lax.fori_loop(0, WIN // TILE, weigh, (zero, zero))
        inv = 1.0 / jnp.sum(denom, axis=0, keepdims=True)
        delta = jnp.sum(mix, axis=0, keepdims=True) * inv

        def finish(i, _):
            rows = pl.ds(pl.multiple_of(i * TILE, TILE), TILE)
            p = scores[rows, lanes] * inv
            probs[rows, lanes] = p.astype(jnp.bfloat16)
            sgrads[rows, lanes] = (p * (vgrads[rows, lanes] - delta)).astype(jnp.bfloat16)
            return 0

        lax.fori_loop(0, WIN // TILE, finish, 0)
        out, h = dq
        grad = (mm(win_t[:QK, :], sgrads[:, lanes]) * SCORE_SCALE).astype(jnp.bfloat16)
        out[h] = grad[:, :BLOCK]
        out[h + 1] = grad[:, BLOCK:]

    trade = []
    for n in (2, 3):
        h = (n - 2) * 2
        query_chunk(n, (dq1, h))
        for k in (h, h + 1):
            copy = remote(dq1.at[k], got_out.at[k], st.at[k], vt.at[k], at_ctx(n_ctx // 2))
            copy.start()
            trade.append(copy)
    keep_own = pltpu.make_async_copy(dq1, own_out, out_sem.at[0])
    keep_own.start()
    query_chunk(0, (dq0, 0))
    query_chunk(1, (dq0, 2))
    keep_first = pltpu.make_async_copy(dq0, dq0_out, out_sem.at[1])
    keep_first.start()

    def key_grads(slot, _):
        rows = pl.ds(pl.multiple_of(slot * TOK, TOK), TOK)
        grads[rows, :] = mm_nt(sgrads[rows, :], q_all[...]) * SCORE_SCALE
        grads[rows, :LAT] += mm(probs[rows, :], g_all[...])
        theirs = pl.ds(pl.multiple_of(slot * TOK + (1 - core) * HALF, HALF), HALF)
        r1_out[pl.ds(pl.multiple_of(slot * HALF, HALF), HALF), :] = grads[theirs, :].astype(jnp.bfloat16)
        return 0

    lax.fori_loop(0, BACK + 1, key_grads, 0)
    swap = remote(r1_out, r1_in, sr1, vr1, sibling)
    swap.start()
    swap.wait_recv()

    for slot in range(BACK + 1):
        ours = pl.ds(pl.multiple_of(slot * TOK + core * HALF, HALF), HALF)
        grads[ours, :] += r1_in[slot * HALF:(slot + 1) * HALF, :].astype(jnp.float32)
    spread = []
    for b in (1, 3, 2):
        to = lax.rem(y + b, n_y)
        for slot in range(BACK + 1):
            rows = pl.ds(pl.multiple_of(slot * TOK + core * HALF + to * PIECE, PIECE), PIECE)
            r2_out[b - 1, slot * PIECE:(slot + 1) * PIECE, :] = grads[rows, :].astype(jnp.bfloat16)
        copy = remote(r2_out.at[b - 1], r2_in.at[b - 1], sr2.at[b - 1], vr2.at[b - 1], at_y(b))
        copy.start()
        spread.append(copy)
    for copy in spread:
        copy.wait_recv()
    sums = []
    for slot in range(BACK + 1):
        rows = pl.ds(pl.multiple_of(slot * TOK + mine, PIECE), PIECE)
        part = grads[rows, :]
        for b in range(3):
            part = part + r2_in[b, slot * PIECE:(slot + 1) * PIECE, :].astype(jnp.float32)
        sums.append(part)

    along = []
    for d in (1, 3, 2):
        r3_out[d - 1] = sums[BACK - d].astype(jnp.bfloat16)
        to = {"ctx": zbase + lax.rem(x - d + 4, 4)}
        copy = remote(r3_out.at[d - 1], r3_in.at[d - 1], sr3.at[d - 1], vr3.at[d - 1], to)
        copy.start()
        along.append(copy)
    for copy in along:
        copy.wait_recv()
    here = sums[BACK]
    before = sums[0]
    for d in (1, 2, 3):
        part = r3_in[d - 1].astype(jnp.float32)
        inside = x + d < 4
        here = here + jnp.where(inside, part, 0.0)
        before = before + jnp.where(inside, 0.0, part)
    r4_out[...] = before.astype(jnp.bfloat16)
    down = remote(r4_out, r4_in, sr4, vr4, at_ctx(-4))
    down.start()
    down.wait_recv()
    lat[...] = (here + r4_in[...].astype(jnp.float32))[:, :QK]
    keep_lat = pltpu.make_async_copy(lat, lat_out, out_sem.at[2])
    keep_lat.start()

    for copy in first + [c for d in hops for c in second[d]] + third + [swap] + spread + along + [down]:
        copy.wait_send()
    keep_own.wait()
    keep_first.wait()
    keep_lat.wait()
    for copy in trade:
        copy.wait_send()
    for copy in trade:
        copy.wait_recv()


def on_device(queries, latent_kv, out_grad, lengths, block_plan):
    bf16, f32, i32 = jnp.bfloat16, jnp.float32, jnp.int32
    any_space = pl.BlockSpec(memory_space=pl.ANY)
    dma = pltpu.SemaphoreType.DMA
    block_shape = (HEADS_DEV, QK, BLOCK)
    vmem = pltpu.VMEM
    first, own, got, latent_grad = pl.pallas_call(
        fused,
        out_shape=[jax.ShapeDtypeStruct(block_shape, bf16)] * 3 + [jax.ShapeDtypeStruct((PIECE, QK), f32)],
        in_specs=[any_space] * 3 + [pl.BlockSpec(memory_space=pltpu.SMEM)],
        out_specs=[any_space] * 4,
        scratch_shapes=[
            vmem((HEADS_DEV, QK, TOK), bf16),
            vmem((QK, TOK), bf16),
            vmem((TOK, HEADS_DEV, LAT), bf16),
            vmem((WIDE, ROWS), bf16),
            vmem((ROWS, LAT), bf16),
            vmem((WIN, WIDE), bf16),
            vmem((WIDE, WIN), bf16),
            vmem((WIN, ROWS), f32),
            vmem((WIN, ROWS), f32),
            vmem((WIN, ROWS), bf16),
            vmem((WIN, ROWS), bf16),
            vmem((8, ROWS), f32),
            vmem((1, ROWS), i32),
            vmem((1, ROWS), i32),
            vmem((WIN, WIDE), f32),
            vmem(block_shape, bf16),
            vmem(block_shape, bf16),
            vmem(((BACK + 1) * HALF, WIDE), bf16),
            vmem(((BACK + 1) * HALF, WIDE), bf16),
            vmem((3, (BACK + 1) * PIECE, WIDE), bf16),
            vmem((3, (BACK + 1) * PIECE, WIDE), bf16),
            vmem((3, PIECE, WIDE), bf16),
            vmem((3, PIECE, WIDE), bf16),
            vmem((PIECE, WIDE), bf16),
            vmem((PIECE, WIDE), bf16),
            vmem((PIECE, QK), f32),
            dma((3,)), dma((3,)),
            dma((4,)), dma((4,)), dma((4, 3)), dma((4, 3)), dma((4,)), dma((4,)),
            dma((4,)), dma((4,)),
            dma, dma, dma((3,)), dma((3,)), dma((3,)), dma((3,)), dma, dma,
        ],
        compiler_params=pltpu.CompilerParams(
            collective_id=0, has_side_effects=True, vmem_limit_bytes=48 * 1024 * 1024
        ),
        cost_estimate=pl.CostEstimate(flops=8_000_000_000, bytes_accessed=8_000_000, transcendentals=1_300_000),
    )(jnp.transpose(queries, (1, 2, 0)), jnp.transpose(latent_kv), out_grad, lengths)

    position = lax.axis_index("ctx")
    blocks_here = TOK // BLOCK
    last_block = position * blocks_here + blocks_here - 1
    holder = jnp.sum(jnp.where(jnp.arange(block_plan.shape[0], dtype=i32) == last_block, block_plan, 0))
    last = jnp.where(holder != position, got, own)
    query_grad = jnp.transpose(jnp.concatenate([first, last], axis=2), (2, 0, 1))
    return query_grad, latent_grad


def solution(mesh):
    return jax.shard_map(
        on_device,
        mesh=mesh,
        in_specs=(P("ctx", "head", None), P("ctx", None), P("ctx", "head", None), P(), P()),
        out_specs=(P("ctx", "head", None), P(("ctx", "head"), None)),
        check_vma=False,
    )
```

```python
import functools

import jax
import jax.numpy as jnp
from jax import lax
from jax.experimental import pallas as pl
from jax.experimental.pallas import tpu as pltpu
from jax.sharding import PartitionSpec as P

BLOCK = 128
SCORE_SCALE = 192.0 ** (-0.5)
MASKED_FILL = -1e30
MESH = pl.DeviceIdType.MESH

HEADS_DEV = 4
TOK = 256
ROWS = TOK * HEADS_DEV
QK = 576
LAT = 512
WIDE = 640
BACK = 4
WIN = (BACK + 1) * TOK
CHUNK = 256
TILE = 128
PIECE = 32
HALF = TOK // 2
FAR = 16
VMEM_BYTES = 63 * 1024 * 1024

NT = (((1,), (1,)), ((), ()))


def mm(a, b):
    return jnp.dot(a, b, preferred_element_type=jnp.float32)


def mm_nt(a, b):
    return lax.dot_general(a, b, NT, preferred_element_type=jnp.float32)


def fused(
    q_hbm, k_hbm, g_hbm, len_ref, plan_ref,
    dq_out, lat_out,
    q_in, k_in, g_in, q_all, g_all, win, win_t, scores, vgrads, probs, sgrads,
    top, start_of, pos_of, grads, dq0, dq1, mid, got,
    r1_out, r1_in, r2_out, r2_in, r3_out, r3_in, r4_out, r4_in, lat,
    in_sem, out_sem, s1, v1, s2, v2, s3, v3, st, vt, su, vu, sr1, vr1, sr2, vr2, sr3, vr3, sr4, vr4,
):
    ctx = lax.axis_index("ctx")
    head = lax.axis_index("head")
    n_ctx = lax.axis_size("ctx")
    n_y = 4
    y = head // 2
    core = head % 2
    x = ctx % 4
    zbase = ctx - x

    def at_ctx(by):
        return {"ctx": lax.rem(ctx + by + n_ctx, n_ctx)}

    def at_y(by):
        return {"head": lax.rem(y + by, n_y) * 2 + core}

    sibling = {"head": y * 2 + (1 - core)}

    peers = [at_ctx(b) for b in (1, 2, 3, 4, -1, -2, -3, -4, FAR, -FAR)]
    peers += [at_y(b) for b in (1, 2, 3)] + [sibling]
    load_k = pltpu.make_async_copy(k_hbm, k_in, in_sem.at[0])
    load_q = pltpu.make_async_copy(q_hbm, q_in, in_sem.at[1])
    load_g = pltpu.make_async_copy(g_hbm, g_in, in_sem.at[2])
    load_k.start()
    load_q.start()
    load_g.start()
    barrier = pltpu.get_barrier_semaphore()
    for peer in peers:
        pl.semaphore_signal(barrier, inc=1, device_id=peer, device_id_type=MESH)
    load_k.wait()

    own0 = BACK * TOK
    keys = jnp.transpose(k_in[...])
    win[pl.ds(own0, TOK), QK:] = jnp.zeros((TOK, WIDE - QK), jnp.bfloat16)
    for c in range(2):
        for yy in range(4):
            at = own0 + c * HALF + yy * PIECE
            frm = yy * 2 * PIECE + c * PIECE
            win[at:at + PIECE, :QK] = keys[frm:frm + PIECE, :]

    mine = core * HALF + y * PIECE
    pl.semaphore_wait(barrier, len(peers))

    def piece(slot, by=0, first=0, size=PIECE):
        at = slot * TOK + core * HALF + lax.rem(y + by, n_y) * PIECE + first
        return win.at[pl.ds(pl.multiple_of(at, 16), size), :]

    def half(slot):
        return win.at[pl.ds(pl.multiple_of(slot * TOK + core * HALF, HALF), HALF), :]

    def remote(src, dst, ss, rs, to):
        return pltpu.make_async_remote_copy(
            src_ref=src, dst_ref=dst, send_sem=ss, recv_sem=rs, device_id=to, device_id_type=MESH
        )

    hops = (4, 1, 3, 2)
    first = [remote(piece(BACK), piece(BACK - d), s1.at[d - 1], v1.at[d - 1], at_ctx(d)) for d in hops]
    for copy in first:
        copy.start()

    load_q.wait()
    q_all[QK:, :] = jnp.zeros((WIDE - QK, ROWS), jnp.bfloat16)
    for b in range(2):
        for h in range(HEADS_DEV):
            at = b * 512 + h * BLOCK
            q_all[:QK, at:at + BLOCK] = q_in[h, :, b * BLOCK:(b + 1) * BLOCK]

    lane = lax.broadcasted_iota(jnp.int32, (1, ROWS), 1)
    q_pos = ctx * TOK + (lane // 512) * BLOCK + lane % BLOCK
    begin = jnp.zeros((1, ROWS), jnp.int32)
    total = jnp.int32(0)
    for d in range(len_ref.shape[0]):
        begin = jnp.where(q_pos >= total, total, begin)
        total = total + len_ref[d]
    pos_of[...] = q_pos
    start_of[...] = begin
    top[...] = jnp.full(top.shape, MASKED_FILL, jnp.float32)

    def tile_scores(slot, lane0, count, width, turn=False):
        rows = pl.ds(pl.multiple_of(slot * TOK, TOK), TOK)
        keys = win[rows, :]
        if turn:
            win_t[:, rows] = jnp.transpose(keys)
        row = lax.broadcasted_iota(jnp.int32, (TOK, width), 0)
        k_pos = (ctx - BACK + slot) * TOK + ((row % HALF) // PIECE) * 2 * PIECE + (row // HALF) * PIECE + row % PIECE

        def chunk(n, _):
            lanes = pl.ds(pl.multiple_of(lane0 + n * width, width), width)
            s = mm(keys, q_all[:, lanes]) * SCORE_SCALE
            allowed = (k_pos >= start_of[:, lanes]) & (k_pos <= pos_of[:, lanes])
            s = jnp.where(allowed, s, MASKED_FILL)
            scores[rows, lanes] = s
            top[:, lanes] = jnp.maximum(top[:, lanes], jnp.max(s.reshape(TOK // 8, 8, width), axis=0))
            vgrads[rows, lanes] = mm_nt(keys[:, :LAT], g_all[lanes, :])
            return 0

        if count == 1:
            chunk(0, 0)
        else:
            lax.fori_loop(0, count, chunk, 0)

    def earlier_scores(lane0, width):
        def step(slot, _):
            tile_scores(slot, lane0, 1, width)
            return 0

        lax.fori_loop(0, BACK, step, 0)

    second, third = {}, {}
    for d in hops:
        slot = BACK - d
        first[hops.index(d)].wait_recv()
        second[d] = [
            remote(piece(slot), piece(slot), s2.at[d - 1, b - 1], v2.at[d - 1, b - 1], at_y(b)) for b in (1, 3, 2)
        ]
        for copy in second[d]:
            copy.start()

    load_g.wait()
    to_row = lax.broadcasted_iota(jnp.int32, (CHUNK, CHUNK), 0)
    from_row = lax.broadcasted_iota(jnp.int32, (CHUNK, CHUNK), 1)
    shuffle = (from_row == (to_row % 64) * HEADS_DEV + to_row // 64).astype(jnp.bfloat16)

    def shuffle_rows(k):
        rows = g_in[k * 64:(k + 1) * 64].reshape(CHUNK, LAT)
        rows = mm(shuffle, rows).astype(jnp.bfloat16)
        for h in range(HEADS_DEV):
            at = (k // 2) * 512 + h * BLOCK + (k % 2) * 64
            g_all[at:at + 64, :] = rows[h * 64:(h + 1) * 64, :]

    for k in range(4):
        shuffle_rows(k)
    tile_scores(BACK, 512, 4, BLOCK, True)
    for i, d in enumerate(hops):
        for copy in second[d]:
            copy.wait_recv()
        third[d] = remote(half(BACK - d), half(BACK - d), s3.at[d - 1], v3.at[d - 1], sibling)
        third[d].start()
        if i == 1:
            tile_scores(BACK, 0, 2, CHUNK)
    for d in hops:
        third[d].wait_recv()
        tile_scores(BACK - d, 512, 1, BLOCK, True)

    def query_chunk(lane0, width, out, h):
        lanes = slice(lane0, lane0 + width)
        peak = jnp.max(top[:, lanes], axis=0, keepdims=True)

        def weigh(i, carry):
            denom, mix = carry
            rows = pl.ds(pl.multiple_of(i * TILE, TILE), TILE)
            p = jnp.exp(scores[rows, lanes] - peak)
            scores[rows, lanes] = p
            pd = p * vgrads[rows, lanes]
            denom = denom + jnp.sum(p.reshape(TILE // 8, 8, width), axis=0)
            mix = mix + jnp.sum(pd.reshape(TILE // 8, 8, width), axis=0)
            return denom, mix

        zero = jnp.zeros((8, width), jnp.float32)
        denom, mix = lax.fori_loop(0, WIN // TILE, weigh, (zero, zero))
        inv = 1.0 / jnp.sum(denom, axis=0, keepdims=True)
        delta = jnp.sum(mix, axis=0, keepdims=True) * inv

        def finish(i, _):
            rows = pl.ds(pl.multiple_of(i * TILE, TILE), TILE)
            p = scores[rows, lanes] * inv
            probs[rows, lanes] = p.astype(jnp.bfloat16)
            sgrads[rows, lanes] = (p * (vgrads[rows, lanes] - delta)).astype(jnp.bfloat16)
            return 0

        lax.fori_loop(0, WIN // TILE, finish, 0)
        grad = (mm(win_t[:QK, :], sgrads[:, lanes]) * SCORE_SCALE).astype(jnp.bfloat16)
        for k in range(width // BLOCK):
            out[h + k] = grad[:, k * BLOCK:(k + 1) * BLOCK]

    ways = ((slice(0, QK // 2), FAR), (slice(QK // 2, QK), -FAR))
    trade = []
    for k in range(HEADS_DEV):
        if k > 0:
            earlier_scores(512 + k * BLOCK, BLOCK)
        query_chunk(512 + k * BLOCK, BLOCK, dq1, k)
        for w, (rows, by) in enumerate(ways):
            copy = remote(dq1.at[k, rows], mid.at[k, rows], st.at[k, w], vt.at[k, w], at_ctx(by))
            copy.start()
            trade.append(copy)
    onward = []

    def pass_on(k):
        for w, (rows, by) in enumerate(ways):
            trade[2 * k + w].wait_recv()
            copy = remote(mid.at[k, rows], got.at[k, rows], su.at[k, w], vu.at[k, w], at_ctx(by))
            copy.start()
            onward.append(copy)

    for n in range(2):
        earlier_scores(n * CHUNK, CHUNK)
        query_chunk(n * CHUNK, CHUNK, dq0, 2 * n)
    keep = [pltpu.make_async_copy(dq0, dq_out.at[:, :, :BLOCK], out_sem.at[0])]
    keep[0].start()

    def key_grads(slot, _):
        rows = pl.ds(pl.multiple_of(slot * TOK, TOK), TOK)
        grads[rows, :] = mm_nt(sgrads[rows, :], q_all[...]) * SCORE_SCALE
        grads[rows, :LAT] += mm(probs[rows, :], g_all[...])
        theirs = pl.ds(pl.multiple_of(slot * TOK + (1 - core) * HALF, HALF), HALF)
        r1_out[pl.ds(pl.multiple_of(slot * HALF, HALF), HALF), :] = grads[theirs, :].astype(jnp.bfloat16)
        return 0

    lax.fori_loop(0, BACK + 1, key_grads, 0)
    swap = remote(r1_out, r1_in, sr1, vr1, sibling)
    swap.start()
    pass_on(0)
    swap.wait_recv()

    for slot in range(BACK + 1):
        ours = pl.ds(pl.multiple_of(slot * TOK + core * HALF, HALF), HALF)
        grads[ours, :] += r1_in[slot * HALF:(slot + 1) * HALF, :].astype(jnp.float32)
    spread = []
    for b in (1, 3, 2):
        to = lax.rem(y + b, n_y)
        for slot in range(BACK + 1):
            rows = pl.ds(pl.multiple_of(slot * TOK + core * HALF + to * PIECE, PIECE), PIECE)
            r2_out[b - 1, slot * PIECE:(slot + 1) * PIECE, :] = grads[rows, :].astype(jnp.bfloat16)
        copy = remote(r2_out.at[b - 1], r2_in.at[b - 1], sr2.at[b - 1], vr2.at[b - 1], at_y(b))
        copy.start()
        spread.append(copy)
    pass_on(1)
    for copy in spread:
        copy.wait_recv()
    sums = []
    for slot in range(BACK + 1):
        rows = pl.ds(pl.multiple_of(slot * TOK + mine, PIECE), PIECE)
        part = grads[rows, :]
        for b in range(3):
            part = part + r2_in[b, slot * PIECE:(slot + 1) * PIECE, :].astype(jnp.float32)
        sums.append(part)

    along = []
    for d in (1, 3, 2):
        r3_out[d - 1] = sums[BACK - d].astype(jnp.bfloat16)
        to = {"ctx": zbase + lax.rem(x - d + 4, 4)}
        copy = remote(r3_out.at[d - 1], r3_in.at[d - 1], sr3.at[d - 1], vr3.at[d - 1], to)
        copy.start()
        along.append(copy)
    pass_on(2)
    for copy in along:
        copy.wait_recv()
    here = sums[BACK]
    before = sums[0]
    for d in (1, 2, 3):
        part = r3_in[d - 1].astype(jnp.float32)
        inside = x + d < 4
        here = here + jnp.where(inside, part, 0.0)
        before = before + jnp.where(inside, 0.0, part)
    r4_out[...] = before.astype(jnp.bfloat16)
    down = remote(r4_out, r4_in, sr4, vr4, at_ctx(-4))
    down.start()
    pass_on(3)
    down.wait_recv()
    lat[...] = (here + r4_in[...].astype(jnp.float32))[:, :QK]
    keep.append(pltpu.make_async_copy(lat, lat_out, out_sem.at[1]))
    keep[1].start()
    sent = first + [c for d in hops for c in second[d] + [third[d]]]
    for copy in sent + [swap] + spread + along + [down] + trade:
        copy.wait_send()
    traded = plan_ref[2 * ctx + 1] != ctx
    for k in range(HEADS_DEV):
        for copy in onward[2 * k:2 * k + 2]:
            copy.wait_recv()
        dq1[k] = jnp.where(traded, got[k], dq1[k])
        keep.append(pltpu.make_async_copy(dq1.at[k], dq_out.at[k, :, BLOCK:], out_sem.at[2 + k]))
        keep[-1].start()
    for copy in onward:
        copy.wait_send()
    for copy in keep:
        copy.wait()


def place(dq_in, lat_in, dq_out, lat_out, dq_held, lat_held, in_sem, out_sem):
    parts = [(dq_in.at[h], dq_held.at[h], dq_out.at[h]) for h in range(HEADS_DEV)] + [(lat_in, lat_held, lat_out)]
    loads = [pltpu.make_async_copy(src, held, in_sem.at[i]) for i, (src, held, _) in enumerate(parts)]
    stores = [pltpu.make_async_copy(held, dst, out_sem.at[i]) for i, (_, held, dst) in enumerate(parts)]
    for load in loads:
        load.start()
    for load, store in zip(loads, stores):
        load.wait()
        store.start()
    for store in stores:
        store.wait()


def on_device(queries, latent_kv, out_grad, lengths, block_plan):
    bf16, f32, i32 = jnp.bfloat16, jnp.float32, jnp.int32
    hbm = pl.BlockSpec(memory_space=pl.ANY)
    smem = pl.BlockSpec(memory_space=pltpu.SMEM)
    dma = pltpu.SemaphoreType.DMA
    block_shape = (HEADS_DEV, QK, BLOCK)
    vmem = pltpu.VMEM
    query_grad, latent_grad = pl.pallas_call(
        fused,
        out_shape=[jax.ShapeDtypeStruct((HEADS_DEV, QK, TOK), bf16), jax.ShapeDtypeStruct((PIECE, QK), f32)],
        in_specs=[hbm] * 3 + [smem] * 2,
        out_specs=[hbm] * 2,
        scratch_shapes=[
            vmem((HEADS_DEV, QK, TOK), bf16),
            vmem((QK, TOK), bf16),
            vmem((TOK, HEADS_DEV, LAT), bf16),
            vmem((WIDE, ROWS), bf16),
            vmem((ROWS, LAT), bf16),
            vmem((WIN, WIDE), bf16),
            vmem((WIDE, WIN), bf16),
            vmem((WIN, ROWS), f32),
            vmem((WIN, ROWS), f32),
            vmem((WIN, ROWS), bf16),
            vmem((WIN, ROWS), bf16),
            vmem((8, ROWS), f32),
            vmem((1, ROWS), i32),
            vmem((1, ROWS), i32),
            vmem((WIN, WIDE), f32),
            vmem(block_shape, bf16),
            vmem(block_shape, bf16),
            vmem(block_shape, bf16),
            vmem(block_shape, bf16),
            vmem(((BACK + 1) * HALF, WIDE), bf16),
            vmem(((BACK + 1) * HALF, WIDE), bf16),
            vmem((3, (BACK + 1) * PIECE, WIDE), bf16),
            vmem((3, (BACK + 1) * PIECE, WIDE), bf16),
            vmem((3, PIECE, WIDE), bf16),
            vmem((3, PIECE, WIDE), bf16),
            vmem((PIECE, WIDE), bf16),
            vmem((PIECE, WIDE), bf16),
            vmem((PIECE, QK), f32),
            dma((3,)), dma((6,)),
            dma((4,)), dma((4,)), dma((4, 3)), dma((4, 3)), dma((4,)), dma((4,)),
            dma((4, 2)), dma((4, 2)), dma((4, 2)), dma((4, 2)),
            dma, dma, dma((3,)), dma((3,)), dma((3,)), dma((3,)), dma, dma,
        ],
        compiler_params=pltpu.CompilerParams(
            collective_id=0, has_side_effects=True, vmem_limit_bytes=VMEM_BYTES
        ),
        cost_estimate=pl.CostEstimate(flops=8_000_000_000, bytes_accessed=8_000_000, transcendentals=1_300_000),
    )(jnp.transpose(queries, (1, 2, 0)), jnp.transpose(latent_kv), out_grad, lengths, block_plan)

    query_grad, latent_grad = pl.pallas_call(
        place,
        out_shape=[jax.ShapeDtypeStruct(query_grad.shape, bf16), jax.ShapeDtypeStruct(latent_grad.shape, f32)],
        in_specs=[hbm] * 2,
        out_specs=[hbm] * 2,
        scratch_shapes=[
            vmem(query_grad.shape, bf16), vmem(latent_grad.shape, f32), dma((HEADS_DEV + 1,)), dma((HEADS_DEV + 1,)),
        ],
        compiler_params=pltpu.CompilerParams(vmem_limit_bytes=VMEM_BYTES),
    )(query_grad, latent_grad)
    return jnp.transpose(query_grad, (2, 0, 1)), latent_grad


def solution(mesh):
    return jax.shard_map(
        on_device,
        mesh=mesh,
        in_specs=(P("ctx", "head", None), P("ctx", None), P("ctx", "head", None), P(), P()),
        out_specs=(P("ctx", "head", None), P(("ctx", "head"), None)),
        check_vma=False,
    )
```

```python
import functools

import jax
import jax.numpy as jnp
from jax import lax
from jax.experimental import pallas as pl
from jax.experimental.pallas import tpu as pltpu
from jax.sharding import PartitionSpec as P

BLOCK = 128
SCORE_SCALE = 192.0 ** (-0.5)
MASKED_FILL = -1e30
MESH = pl.DeviceIdType.MESH

HEADS_DEV = 4
TOK = 256
ROWS = TOK * HEADS_DEV
QK = 576
LAT = 512
WIDE = 640
BACK = 4
WIN = (BACK + 1) * TOK
CHUNK = 256
TILE = 128
STRIP = QK // 4
PIECE = 32
HALF = TOK // 2
FAR = 16
VMEM_BYTES = 63 * 1024 * 1024

NT = (((1,), (1,)), ((), ()))


def mm(a, b):
    return jnp.dot(a, b, preferred_element_type=jnp.float32)


def mm_nt(a, b):
    return lax.dot_general(a, b, NT, preferred_element_type=jnp.float32)


def fused(
    q_hbm, k_hbm, g_hbm, len_ref, plan_ref,
    dq_out, lat_out,
    q_in, g_in, q_all, g_all, win, win_t, scores, vgrads, probs, sgrads,
    top, start_of, pos_of, grads, dq0, dq1, mid, got,
    r1_out, r1_in, r2_out, r2_in, r3_out, r3_in, r4_out, r4_in, lat,
    in_sem, out_sem, s1, v1, sx, vx, s2, v2, s3, v3, st, vt, su, vu, sr1, vr1, sr2, vr2, sr3, vr3, sr4, vr4,
):
    ctx = lax.axis_index("ctx")
    head = lax.axis_index("head")
    n_ctx = lax.axis_size("ctx")
    n_y = 4
    y = head // 2
    core = head % 2
    x = ctx % 4
    zbase = ctx - x

    def at_ctx(by):
        return {"ctx": lax.rem(ctx + by + n_ctx, n_ctx)}

    def at_y(by):
        return {"head": lax.rem(y + by, n_y) * 2 + core}

    sibling = {"head": y * 2 + (1 - core)}

    peers = [at_ctx(b) for b in (1, 2, 3, 4, -1, -2, -3, -4, FAR, -FAR)]
    peers += [at_y(b) for b in (1, 2, 3)] + [sibling]
    own_at = BACK * TOK
    load_k = pltpu.make_async_copy(k_hbm, win_t.at[pl.ds(0, QK), pl.ds(own_at, TOK)], in_sem.at[0])
    load_q = pltpu.make_async_copy(q_hbm, q_in, in_sem.at[1])
    load_g = pltpu.make_async_copy(g_hbm, g_in, in_sem.at[2])
    load_k.start()
    load_q.start()
    load_g.start()
    barrier = pltpu.get_barrier_semaphore()
    for peer in peers:
        pl.semaphore_signal(barrier, inc=1, device_id=peer, device_id_type=MESH)
    win_t[QK:, :] = jnp.zeros((WIDE - QK, WIN), jnp.bfloat16)
    pl.semaphore_wait(barrier, len(peers))
    keys_of_core = pl.ds(pl.multiple_of(core * HALF, HALF), HALF)
    columns = pl.ds(pl.multiple_of(y * STRIP, 16), STRIP)

    def half(slot):
        return win_t.at[pl.ds(0, QK), pl.ds(pl.multiple_of(slot * TOK + core * HALF, HALF), HALF)]

    def piece(slot):
        return win_t.at[columns, pl.ds(pl.multiple_of(slot * TOK + core * HALF, HALF), HALF)]

    def remote(src, dst, ss, rs, to):
        return pltpu.make_async_remote_copy(
            src_ref=src, dst_ref=dst, send_sem=ss, recv_sem=rs, device_id=to, device_id_type=MESH
        )

    hops = (1, 3, 2)
    beside = {d: remote(k_hbm.at[columns, keys_of_core], piece(BACK - d), sx.at[d - 1], vx.at[d - 1], at_ctx(d)) for d in hops}
    for d in hops:
        beside[d].start()
    up = [remote(k_hbm.at[:, keys_of_core], half(0), s1, v1, at_ctx(BACK))]

    load_q.wait()
    q_all[QK:, :] = jnp.zeros((WIDE - QK, ROWS), jnp.bfloat16)
    for b in range(2):
        for h in range(HEADS_DEV):
            at = b * 512 + h * BLOCK
            q_all[:QK, at:at + BLOCK] = q_in[h, :, b * BLOCK:(b + 1) * BLOCK]

    lane = lax.broadcasted_iota(jnp.int32, (1, ROWS), 1)
    q_pos = ctx * TOK + (lane // 512) * BLOCK + lane % BLOCK
    begin = jnp.zeros((1, ROWS), jnp.int32)
    total = jnp.int32(0)
    for d in range(len_ref.shape[0]):
        begin = jnp.where(q_pos >= total, total, begin)
        total = total + len_ref[d]
    pos_of[...] = q_pos
    start_of[...] = begin
    top[...] = jnp.full(top.shape, MASKED_FILL, jnp.float32)

    def tile_scores(slot, lane0, count, width, turn=False):
        rows = pl.ds(pl.multiple_of(slot * TOK, TOK), TOK)
        if turn:
            keys = jnp.transpose(win_t[:, rows])
            win[rows, :] = keys
        else:
            keys = win[rows, :]
        row = lax.broadcasted_iota(jnp.int32, (TOK, width), 0)
        k_pos = (ctx - BACK + slot) * TOK + row

        def chunk(n, _):
            lanes = pl.ds(pl.multiple_of(lane0 + n * width, width), width)
            s = mm(keys, q_all[:, lanes]) * SCORE_SCALE
            allowed = (k_pos >= start_of[:, lanes]) & (k_pos <= pos_of[:, lanes])
            s = jnp.where(allowed, s, MASKED_FILL)
            scores[rows, lanes] = s
            top[:, lanes] = jnp.maximum(top[:, lanes], jnp.max(s.reshape(TOK // 8, 8, width), axis=0))
            vgrads[rows, lanes] = mm_nt(keys[:, :LAT], g_all[lanes, :])
            return 0

        if count == 1:
            chunk(0, 0)
        else:
            lax.fori_loop(0, count, chunk, 0)

    def earlier_scores(lane0, width):
        def step(slot, _):
            tile_scores(slot, lane0, 1, width)
            return 0

        lax.fori_loop(0, BACK, step, 0)

    second, third = {}, {}
    for d in hops:
        slot = BACK - d
        beside[d].wait_recv()
        second[d] = [
            remote(piece(slot), piece(slot), s2.at[d - 1, b - 1], v2.at[d - 1, b - 1], at_y(b)) for b in (1, 3, 2)
        ]
        for copy in second[d]:
            copy.start()
        if d == hops[0]:
            for copy in up:
                copy.start()

    load_g.wait()
    to_row = lax.broadcasted_iota(jnp.int32, (CHUNK, CHUNK), 0)
    from_row = lax.broadcasted_iota(jnp.int32, (CHUNK, CHUNK), 1)
    shuffle = (from_row == (to_row % 64) * HEADS_DEV + to_row // 64).astype(jnp.bfloat16)

    def shuffle_rows(k):
        rows = g_in[k * 64:(k + 1) * 64].reshape(CHUNK, LAT)
        rows = mm(shuffle, rows).astype(jnp.bfloat16)
        for h in range(HEADS_DEV):
            at = (k // 2) * 512 + h * BLOCK + (k % 2) * 64
            g_all[at:at + 64, :] = rows[h * 64:(h + 1) * 64, :]

    for k in range(4):
        shuffle_rows(k)
    load_k.wait()
    tile_scores(BACK, 512, 4, BLOCK, True)
    def exchange(slot):
        third[slot] = remote(half(slot), half(slot), s3.at[slot], v3.at[slot], sibling)
        third[slot].start()

    for d in hops:
        for copy in second[d]:
            copy.wait_recv()
        exchange(BACK - d)
        if d == hops[0]:
            for copy in up:
                copy.wait_recv()
            exchange(0)
    for slot in (BACK - hops[0], 0, BACK - hops[1], BACK - hops[2]):
        third[slot].wait_recv()
        tile_scores(slot, 512, 1, BLOCK, True)

    def query_chunk(lane0, width, out, h):
        lanes = slice(lane0, lane0 + width)
        peak = jnp.max(top[:, lanes], axis=0, keepdims=True)

        def weigh(i, carry):
            denom, mix = carry
            rows = pl.ds(pl.multiple_of(i * TILE, TILE), TILE)
            p = jnp.exp(scores[rows, lanes] - peak)
            scores[rows, lanes] = p
            pd = p * vgrads[rows, lanes]
            denom = denom + jnp.sum(p.reshape(TILE // 8, 8, width), axis=0)
            mix = mix + jnp.sum(pd.reshape(TILE // 8, 8, width), axis=0)
            return denom, mix

        zero = jnp.zeros((8, width), jnp.float32)
        denom, mix = lax.fori_loop(0, WIN // TILE, weigh, (zero, zero))
        inv = 1.0 / jnp.sum(denom, axis=0, keepdims=True)
        delta = jnp.sum(mix, axis=0, keepdims=True) * inv

        def finish(i, _):
            rows = pl.ds(pl.multiple_of(i * TILE, TILE), TILE)
            p = scores[rows, lanes] * inv
            probs[rows, lanes] = p.astype(jnp.bfloat16)
            sgrads[rows, lanes] = (p * (vgrads[rows, lanes] - delta)).astype(jnp.bfloat16)
            return 0

        lax.fori_loop(0, WIN // TILE, finish, 0)
        grad = (mm(win_t[:QK, :], sgrads[:, lanes]) * SCORE_SCALE).astype(jnp.bfloat16)
        for k in range(width // BLOCK):
            out[h + k] = grad[:, k * BLOCK:(k + 1) * BLOCK]

    ways = ((slice(0, QK // 2), FAR), (slice(QK // 2, QK), -FAR))
    trade = []
    for k in range(HEADS_DEV):
        if k > 0:
            earlier_scores(512 + k * BLOCK, BLOCK)
        query_chunk(512 + k * BLOCK, BLOCK, dq1, k)
        for w, (rows, by) in enumerate(ways):
            copy = remote(dq1.at[k, rows], mid.at[k, rows], st.at[k, w], vt.at[k, w], at_ctx(by))
            copy.start()
            trade.append(copy)
    onward = []

    def pass_on(k):
        for w, (rows, by) in enumerate(ways):
            trade[2 * k + w].wait_recv()
            copy = remote(mid.at[k, rows], got.at[k, rows], su.at[k, w], vu.at[k, w], at_ctx(by))
            copy.start()
            onward.append(copy)

    for n in range(2):
        tile_scores(BACK, n * CHUNK, 1, CHUNK)
        earlier_scores(n * CHUNK, CHUNK)
        query_chunk(n * CHUNK, CHUNK, dq0, 2 * n)
    keep = [pltpu.make_async_copy(dq0, dq_out.at[:, :, :BLOCK], out_sem.at[0])]
    keep[0].start()

    def owned(slot, of_y, of_core):
        return pl.ds(pl.multiple_of(slot * TOK + of_y * 2 * PIECE + of_core * PIECE, PIECE), PIECE)

    def key_grads(slot, _):
        rows = pl.ds(pl.multiple_of(slot * TOK, TOK), TOK)
        grads[rows, :] = mm_nt(sgrads[rows, :], q_all[...]) * SCORE_SCALE
        grads[rows, :LAT] += mm(probs[rows, :], g_all[...])
        for yy in range(n_y):
            held = pl.ds(pl.multiple_of(slot * HALF + yy * PIECE, PIECE), PIECE)
            r1_out[held, :] = grads[owned(slot, yy, 1 - core), :].astype(jnp.bfloat16)
        return 0

    lax.fori_loop(0, BACK + 1, key_grads, 0)
    swap = remote(r1_out, r1_in, sr1, vr1, sibling)
    swap.start()
    pass_on(0)
    swap.wait_recv()

    def join(slot, _):
        for yy in range(n_y):
            held = pl.ds(pl.multiple_of(slot * HALF + yy * PIECE, PIECE), PIECE)
            grads[owned(slot, yy, core), :] += r1_in[held, :].astype(jnp.float32)
        return 0

    lax.fori_loop(0, BACK + 1, join, 0)
    spread = []
    for b in (1, 3, 2):
        to = lax.rem(y + b, n_y)
        for slot in range(BACK + 1):
            r2_out[b - 1, slot * PIECE:(slot + 1) * PIECE, :] = grads[owned(slot, to, core), :].astype(jnp.bfloat16)
        copy = remote(r2_out.at[b - 1], r2_in.at[b - 1], sr2.at[b - 1], vr2.at[b - 1], at_y(b))
        copy.start()
        spread.append(copy)
    pass_on(1)
    for copy in spread:
        copy.wait_recv()
    sums = []
    for slot in range(BACK + 1):
        part = grads[owned(slot, y, core), :]
        for b in range(3):
            part = part + r2_in[b, slot * PIECE:(slot + 1) * PIECE, :].astype(jnp.float32)
        sums.append(part)

    along = []
    for d in (1, 3, 2):
        r3_out[d - 1] = sums[BACK - d].astype(jnp.bfloat16)
        to = {"ctx": zbase + lax.rem(x - d + 4, 4)}
        copy = remote(r3_out.at[d - 1], r3_in.at[d - 1], sr3.at[d - 1], vr3.at[d - 1], to)
        copy.start()
        along.append(copy)
    pass_on(2)
    for copy in along:
        copy.wait_recv()
    here = sums[BACK]
    before = sums[0]
    for d in (1, 2, 3):
        part = r3_in[d - 1].astype(jnp.float32)
        inside = x + d < 4
        here = here + jnp.where(inside, part, 0.0)
        before = before + jnp.where(inside, 0.0, part)
    r4_out[...] = before.astype(jnp.bfloat16)
    down = remote(r4_out, r4_in, sr4, vr4, at_ctx(-4))
    down.start()
    pass_on(3)
    down.wait_recv()
    lat[...] = (here + r4_in[...].astype(jnp.float32))[:, :QK]
    keep.append(pltpu.make_async_copy(lat, lat_out, out_sem.at[1]))
    keep[1].start()
    sent = up + [c for d in hops for c in second[d] + [beside[d]]] + [third[slot] for slot in range(BACK)]
    for copy in sent + [swap] + spread + along + [down] + trade:
        copy.wait_send()
    traded = plan_ref[2 * ctx + 1] != ctx
    for k in range(HEADS_DEV):
        for copy in onward[2 * k:2 * k + 2]:
            copy.wait_recv()
        dq1[k] = jnp.where(traded, got[k], dq1[k])
        keep.append(pltpu.make_async_copy(dq1.at[k], dq_out.at[k, :, BLOCK:], out_sem.at[2 + k]))
        keep[-1].start()
    for copy in onward:
        copy.wait_send()
    for copy in keep:
        copy.wait()


def place(dq_in, lat_in, dq_out, lat_out, dq_held, lat_held, in_sem, out_sem):
    parts = [(dq_in.at[h], dq_held.at[h], dq_out.at[h]) for h in range(HEADS_DEV)] + [(lat_in, lat_held, lat_out)]
    loads = [pltpu.make_async_copy(src, held, in_sem.at[i]) for i, (src, held, _) in enumerate(parts)]
    stores = [pltpu.make_async_copy(held, dst, out_sem.at[i]) for i, (_, held, dst) in enumerate(parts)]
    for load in loads:
        load.start()
    for load, store in zip(loads, stores):
        load.wait()
        store.start()
    for store in stores:
        store.wait()


def on_device(queries, latent_kv, out_grad, lengths, block_plan):
    bf16, f32, i32 = jnp.bfloat16, jnp.float32, jnp.int32
    hbm = pl.BlockSpec(memory_space=pl.ANY)
    smem = pl.BlockSpec(memory_space=pltpu.SMEM)
    dma = pltpu.SemaphoreType.DMA
    block_shape = (HEADS_DEV, QK, BLOCK)
    vmem = pltpu.VMEM
    query_grad, latent_grad = pl.pallas_call(
        fused,
        out_shape=[jax.ShapeDtypeStruct((HEADS_DEV, QK, TOK), bf16), jax.ShapeDtypeStruct((PIECE, QK), f32)],
        in_specs=[hbm] * 3 + [smem] * 2,
        out_specs=[hbm] * 2,
        scratch_shapes=[
            vmem((HEADS_DEV, QK, TOK), bf16),
            vmem((TOK, HEADS_DEV, LAT), bf16),
            vmem((WIDE, ROWS), bf16),
            vmem((ROWS, LAT), bf16),
            vmem((WIN, WIDE), bf16),
            vmem((WIDE, WIN), bf16),
            vmem((WIN, ROWS), f32),
            vmem((WIN, ROWS), f32),
            vmem((WIN, ROWS), bf16),
            vmem((WIN, ROWS), bf16),
            vmem((8, ROWS), f32),
            vmem((1, ROWS), i32),
            vmem((1, ROWS), i32),
            vmem((WIN, WIDE), f32),
            vmem(block_shape, bf16),
            vmem(block_shape, bf16),
            vmem(block_shape, bf16),
            vmem(block_shape, bf16),
            vmem(((BACK + 1) * HALF, WIDE), bf16),
            vmem(((BACK + 1) * HALF, WIDE), bf16),
            vmem((3, (BACK + 1) * PIECE, WIDE), bf16),
            vmem((3, (BACK + 1) * PIECE, WIDE), bf16),
            vmem((3, PIECE, WIDE), bf16),
            vmem((3, PIECE, WIDE), bf16),
            vmem((PIECE, WIDE), bf16),
            vmem((PIECE, WIDE), bf16),
            vmem((PIECE, QK), f32),
            dma((3,)), dma((6,)),
            dma, dma, dma((3,)), dma((3,)), dma((3, 3)), dma((3, 3)), dma((4,)), dma((4,)),
            dma((4, 2)), dma((4, 2)), dma((4, 2)), dma((4, 2)),
            dma, dma, dma((3,)), dma((3,)), dma((3,)), dma((3,)), dma, dma,
        ],
        compiler_params=pltpu.CompilerParams(
            collective_id=0, has_side_effects=True, vmem_limit_bytes=VMEM_BYTES
        ),
        cost_estimate=pl.CostEstimate(flops=8_000_000_000, bytes_accessed=8_000_000, transcendentals=1_300_000),
    )(jnp.transpose(queries, (1, 2, 0)), jnp.transpose(latent_kv), out_grad, lengths, block_plan)

    query_grad, latent_grad = pl.pallas_call(
        place,
        out_shape=[jax.ShapeDtypeStruct(query_grad.shape, bf16), jax.ShapeDtypeStruct(latent_grad.shape, f32)],
        in_specs=[hbm] * 2,
        out_specs=[hbm] * 2,
        scratch_shapes=[
            vmem(query_grad.shape, bf16), vmem(latent_grad.shape, f32), dma((HEADS_DEV + 1,)), dma((HEADS_DEV + 1,)),
        ],
        compiler_params=pltpu.CompilerParams(vmem_limit_bytes=VMEM_BYTES),
    )(query_grad, latent_grad)
    return jnp.transpose(query_grad, (2, 0, 1)), latent_grad


def solution(mesh):
    return jax.shard_map(
        on_device,
        mesh=mesh,
        in_specs=(P("ctx", "head", None), P("ctx", None), P("ctx", "head", None), P(), P()),
        out_specs=(P("ctx", "head", None), P(("ctx", "head"), None)),
        check_vma=False,
    )
```

```python
import functools

import jax
import jax.numpy as jnp
from jax import lax
from jax.experimental import pallas as pl
from jax.experimental.pallas import tpu as pltpu
from jax.sharding import PartitionSpec as P

BLOCK = 128
SCORE_SCALE = 192.0 ** (-0.5)
MASKED_FILL = -1e30
MESH = pl.DeviceIdType.MESH

HEADS_DEV = 4
TOK = 256
ROWS = TOK * HEADS_DEV
QK = 576
LAT = 512
WIDE = 640
BACK = 4
WIN = (BACK + 1) * TOK
CHUNK = 256
TILE = 128
STRIP = QK // 4
PIECE = 32
HALF = TOK // 2
FAR = 16
VMEM_BYTES = 63 * 1024 * 1024

NT = (((1,), (1,)), ((), ()))


def mm(a, b):
    return jnp.dot(a, b, preferred_element_type=jnp.float32)


def mm_nt(a, b):
    return lax.dot_general(a, b, NT, preferred_element_type=jnp.float32)


def fused(
    q_hbm, k_hbm, g_hbm, len_ref, plan_ref,
    dq_out, lat_out,
    q_in, g_in, q_all, g_all, win, win_t, scores, vgrads, probs, sgrads,
    top, start_of, pos_of, grads, dq0, dq1, mid, got,
    r1_out, r1_in, r2_out, r2_in, r3_out, r3_in, r4_out, r4_in, lat,
    in_sem, out_sem, s1, v1, sx, vx, s2, v2, s3, v3, st, vt, su, vu, sr1, vr1, sr2, vr2, sr3, vr3, sr4, vr4,
):
    ctx = lax.axis_index("ctx")
    head = lax.axis_index("head")
    n_ctx = lax.axis_size("ctx")
    n_y = 4
    y = head // 2
    core = head % 2
    x = ctx % 4
    zbase = ctx - x

    def at_ctx(by):
        return {"ctx": lax.rem(ctx + by + n_ctx, n_ctx)}

    def at_y(by):
        return {"head": lax.rem(y + by, n_y) * 2 + core}

    sibling = {"head": y * 2 + (1 - core)}

    peers = [at_ctx(b) for b in (1, 2, 3, 4, -1, -2, -3, -4, FAR, -FAR)]
    peers += [at_y(b) for b in (1, 2, 3)] + [sibling]
    own_at = BACK * TOK
    load_k = pltpu.make_async_copy(k_hbm, win_t.at[pl.ds(0, QK), pl.ds(own_at, TOK)], in_sem.at[0])
    load_q = pltpu.make_async_copy(q_hbm, q_in, in_sem.at[1])
    load_g = pltpu.make_async_copy(g_hbm, g_in, in_sem.at[2])
    load_k.start()
    load_q.start()
    load_g.start()
    barrier = pltpu.get_barrier_semaphore()
    for peer in peers:
        pl.semaphore_signal(barrier, inc=1, device_id=peer, device_id_type=MESH)
    win_t[QK:, :] = jnp.zeros((WIDE - QK, WIN), jnp.bfloat16)
    pl.semaphore_wait(barrier, len(peers))
    keys_of_core = pl.ds(pl.multiple_of(core * HALF, HALF), HALF)
    columns = pl.ds(pl.multiple_of(y * STRIP, 16), STRIP)

    def half(slot):
        return win_t.at[pl.ds(0, QK), pl.ds(pl.multiple_of(slot * TOK + core * HALF, HALF), HALF)]

    def piece(slot):
        return win_t.at[columns, pl.ds(pl.multiple_of(slot * TOK + core * HALF, HALF), HALF)]

    def remote(src, dst, ss, rs, to):
        return pltpu.make_async_remote_copy(
            src_ref=src, dst_ref=dst, send_sem=ss, recv_sem=rs, device_id=to, device_id_type=MESH
        )

    hops = (1, 3, 2)
    beside = {d: remote(k_hbm.at[columns, keys_of_core], piece(BACK - d), sx.at[d - 1], vx.at[d - 1], at_ctx(d)) for d in hops}
    for d in hops:
        beside[d].start()
    up = [remote(k_hbm.at[:, keys_of_core], half(0), s1, v1, at_ctx(BACK))]

    load_q.wait()
    q_all[QK:, :] = jnp.zeros((WIDE - QK, ROWS), jnp.bfloat16)
    for b in range(2):
        for h in range(HEADS_DEV):
            at = b * 512 + h * BLOCK
            q_all[:QK, at:at + BLOCK] = q_in[h, :, b * BLOCK:(b + 1) * BLOCK]

    lane = lax.broadcasted_iota(jnp.int32, (1, ROWS), 1)
    q_pos = ctx * TOK + (lane // 512) * BLOCK + lane % BLOCK
    begin = jnp.zeros((1, ROWS), jnp.int32)
    total = jnp.int32(0)
    for d in range(len_ref.shape[0]):
        begin = jnp.where(q_pos >= total, total, begin)
        total = total + len_ref[d]
    pos_of[...] = q_pos
    start_of[...] = begin
    top[...] = jnp.full(top.shape, MASKED_FILL, jnp.float32)

    def tile_scores(slot, lane0, count, width, turn=False):
        rows = pl.ds(pl.multiple_of(slot * TOK, TOK), TOK)
        if turn:
            keys = jnp.transpose(win_t[:, rows])
            win[rows, :] = keys
        else:
            keys = win[rows, :]
        row = lax.broadcasted_iota(jnp.int32, (TOK, width), 0)
        k_pos = (ctx - BACK + slot) * TOK + row

        def chunk(n, _):
            lanes = pl.ds(pl.multiple_of(lane0 + n * width, width), width)
            s = mm(keys, q_all[:, lanes]) * SCORE_SCALE
            allowed = (k_pos >= start_of[:, lanes]) & (k_pos <= pos_of[:, lanes])
            s = jnp.where(allowed, s, MASKED_FILL)
            scores[rows, lanes] = s
            top[:, lanes] = jnp.maximum(top[:, lanes], jnp.max(s.reshape(TOK // 8, 8, width), axis=0))
            vgrads[rows, lanes] = mm_nt(keys[:, :LAT], g_all[lanes, :])
            return 0

        if count == 1:
            chunk(0, 0)
        else:
            lax.fori_loop(0, count, chunk, 0)

    def earlier_scores(lane0, width):
        def step(slot, _):
            tile_scores(slot, lane0, 1, width)
            return 0

        lax.fori_loop(0, BACK, step, 0)

    second, third = {}, {}
    for d in hops:
        slot = BACK - d
        beside[d].wait_recv()
        second[d] = [
            remote(piece(slot), piece(slot), s2.at[d - 1, b - 1], v2.at[d - 1, b - 1], at_y(b)) for b in (1, 3, 2)
        ]
        for copy in second[d]:
            copy.start()
        if d == hops[0]:
            for copy in up:
                copy.start()

    load_g.wait()
    to_row = lax.broadcasted_iota(jnp.int32, (CHUNK, CHUNK), 0)
    from_row = lax.broadcasted_iota(jnp.int32, (CHUNK, CHUNK), 1)
    shuffle = (from_row == (to_row % 64) * HEADS_DEV + to_row // 64).astype(jnp.bfloat16)

    def shuffle_rows(k):
        rows = g_in[k * 64:(k + 1) * 64].reshape(CHUNK, LAT)
        rows = mm(shuffle, rows).astype(jnp.bfloat16)
        for h in range(HEADS_DEV):
            at = (k // 2) * 512 + h * BLOCK + (k % 2) * 64
            g_all[at:at + 64, :] = rows[h * 64:(h + 1) * 64, :]

    for k in range(4):
        shuffle_rows(k)
    load_k.wait()
    tile_scores(BACK, 512, 4, BLOCK, True)
    def exchange(slot):
        third[slot] = remote(half(slot), half(slot), s3.at[slot], v3.at[slot], sibling)
        third[slot].start()

    for d in hops:
        for copy in second[d]:
            copy.wait_recv()
        exchange(BACK - d)
        if d == hops[0]:
            for copy in up:
                copy.wait_recv()
            exchange(0)
    for slot in (BACK - hops[0], 0, BACK - hops[1], BACK - hops[2]):
        third[slot].wait_recv()
        tile_scores(slot, 512, 1, BLOCK, True)

    def query_chunk(lane0, width, out, h):
        lanes = slice(lane0, lane0 + width)
        tile = TILE * CHUNK // width
        peak = jnp.max(top[:, lanes], axis=0, keepdims=True)

        def weigh(i, carry):
            denom, mix = carry
            rows = pl.ds(pl.multiple_of(i * tile, tile), tile)
            p = jnp.exp(scores[rows, lanes] - peak)
            scores[rows, lanes] = p
            pd = p * vgrads[rows, lanes]
            denom = denom + jnp.sum(p.reshape(tile // 8, 8, width), axis=0)
            mix = mix + jnp.sum(pd.reshape(tile // 8, 8, width), axis=0)
            return denom, mix

        zero = jnp.zeros((8, width), jnp.float32)
        denom, mix = lax.fori_loop(0, WIN // tile, weigh, (zero, zero))
        inv = 1.0 / jnp.sum(denom, axis=0, keepdims=True)
        delta = jnp.sum(mix, axis=0, keepdims=True) * inv

        def finish(i, _):
            rows = pl.ds(pl.multiple_of(i * tile, tile), tile)
            p = scores[rows, lanes] * inv
            probs[rows, lanes] = p.astype(jnp.bfloat16)
            sgrads[rows, lanes] = (p * (vgrads[rows, lanes] - delta)).astype(jnp.bfloat16)
            return 0

        lax.fori_loop(0, WIN // tile, finish, 0)
        grad = (mm(win_t[:QK, :], sgrads[:, lanes]) * SCORE_SCALE).astype(jnp.bfloat16)
        for k in range(width // BLOCK):
            out[h + k] = grad[:, k * BLOCK:(k + 1) * BLOCK]

    ways = ((slice(0, QK // 2), FAR), (slice(QK // 2, QK), -FAR))
    trade = []
    for k in range(HEADS_DEV):
        if k > 0:
            earlier_scores(512 + k * BLOCK, BLOCK)
        query_chunk(512 + k * BLOCK, BLOCK, dq1, k)
        for w, (rows, by) in enumerate(ways):
            copy = remote(dq1.at[k, rows], mid.at[k, rows], st.at[k, w], vt.at[k, w], at_ctx(by))
            copy.start()
            trade.append(copy)
    onward = []

    def pass_on(k):
        for w, (rows, by) in enumerate(ways):
            trade[2 * k + w].wait_recv()
            copy = remote(mid.at[k, rows], got.at[k, rows], su.at[k, w], vu.at[k, w], at_ctx(by))
            copy.start()
            onward.append(copy)

    for n in range(2):
        tile_scores(BACK, n * CHUNK, 1, CHUNK)
        earlier_scores(n * CHUNK, CHUNK)
        query_chunk(n * CHUNK, CHUNK, dq0, 2 * n)
    keep = [pltpu.make_async_copy(dq0, dq_out.at[:, :, :BLOCK], out_sem.at[0])]
    keep[0].start()

    def owned(slot, of_y, of_core):
        return pl.ds(pl.multiple_of(slot * TOK + of_y * 2 * PIECE + of_core * PIECE, PIECE), PIECE)

    def key_grads(slot, _):
        rows = pl.ds(pl.multiple_of(slot * TOK, TOK), TOK)
        grads[rows, :] = mm_nt(sgrads[rows, :], q_all[...]) * SCORE_SCALE
        grads[rows, :LAT] += mm(probs[rows, :], g_all[...])
        for yy in range(n_y):
            held = pl.ds(pl.multiple_of(slot * HALF + yy * PIECE, PIECE), PIECE)
            r1_out[held, :] = grads[owned(slot, yy, 1 - core), :].astype(jnp.bfloat16)
        return 0

    lax.fori_loop(0, BACK + 1, key_grads, 0)
    swap = remote(r1_out, r1_in, sr1, vr1, sibling)
    swap.start()
    swap.wait_recv()

    def join(slot, _):
        for yy in range(n_y):
            held = pl.ds(pl.multiple_of(slot * HALF + yy * PIECE, PIECE), PIECE)
            grads[owned(slot, yy, core), :] += r1_in[held, :].astype(jnp.float32)
        return 0

    lax.fori_loop(0, BACK + 1, join, 0)
    spread = []
    for b in (1, 3, 2):
        to = lax.rem(y + b, n_y)
        for slot in range(BACK + 1):
            r2_out[b - 1, slot * PIECE:(slot + 1) * PIECE, :] = grads[owned(slot, to, core), :].astype(jnp.bfloat16)
        copy = remote(r2_out.at[b - 1], r2_in.at[b - 1], sr2.at[b - 1], vr2.at[b - 1], at_y(b))
        copy.start()
        spread.append(copy)
    pass_on(0)
    pass_on(1)
    for copy in spread:
        copy.wait_recv()
    sums = []
    for slot in range(BACK + 1):
        part = grads[owned(slot, y, core), :]
        for b in range(3):
            part = part + r2_in[b, slot * PIECE:(slot + 1) * PIECE, :].astype(jnp.float32)
        sums.append(part)

    along = []
    for d in (1, 3, 2):
        r3_out[d - 1] = sums[BACK - d].astype(jnp.bfloat16)
        to = {"ctx": zbase + lax.rem(x - d + 4, 4)}
        copy = remote(r3_out.at[d - 1], r3_in.at[d - 1], sr3.at[d - 1], vr3.at[d - 1], to)
        copy.start()
        along.append(copy)
    pass_on(2)
    for copy in along:
        copy.wait_recv()
    here = sums[BACK]
    before = sums[0]
    for d in (1, 2, 3):
        part = r3_in[d - 1].astype(jnp.float32)
        inside = x + d < 4
        here = here + jnp.where(inside, part, 0.0)
        before = before + jnp.where(inside, 0.0, part)
    r4_out[...] = before.astype(jnp.bfloat16)
    down = remote(r4_out, r4_in, sr4, vr4, at_ctx(-4))
    down.start()
    pass_on(3)
    down.wait_recv()
    lat[...] = (here + r4_in[...].astype(jnp.float32))[:, :QK]
    keep.append(pltpu.make_async_copy(lat, lat_out, out_sem.at[1]))
    keep[1].start()
    sent = up + [c for d in hops for c in second[d] + [beside[d]]] + [third[slot] for slot in range(BACK)]
    for copy in sent + [swap] + spread + along + [down] + trade:
        copy.wait_send()
    traded = plan_ref[2 * ctx + 1] != ctx
    for k in range(HEADS_DEV):
        for copy in onward[2 * k:2 * k + 2]:
            copy.wait_recv()
        dq1[k] = jnp.where(traded, got[k], dq1[k])
        keep.append(pltpu.make_async_copy(dq1.at[k], dq_out.at[k, :, BLOCK:], out_sem.at[2 + k]))
        keep[-1].start()
    for copy in onward:
        copy.wait_send()
    for copy in keep:
        copy.wait()


def place(dq_in, lat_in, dq_out, lat_out, dq_held, lat_held, in_sem, out_sem):
    parts = [(dq_in.at[h], dq_held.at[h], dq_out.at[h]) for h in range(HEADS_DEV)] + [(lat_in, lat_held, lat_out)]
    loads = [pltpu.make_async_copy(src, held, in_sem.at[i]) for i, (src, held, _) in enumerate(parts)]
    stores = [pltpu.make_async_copy(held, dst, out_sem.at[i]) for i, (_, held, dst) in enumerate(parts)]
    for load in loads:
        load.start()
    for load, store in zip(loads, stores):
        load.wait()
        store.start()
    for store in stores:
        store.wait()


def on_device(queries, latent_kv, out_grad, lengths, block_plan):
    bf16, f32, i32 = jnp.bfloat16, jnp.float32, jnp.int32
    hbm = pl.BlockSpec(memory_space=pl.ANY)
    smem = pl.BlockSpec(memory_space=pltpu.SMEM)
    dma = pltpu.SemaphoreType.DMA
    block_shape = (HEADS_DEV, QK, BLOCK)
    vmem = pltpu.VMEM
    query_grad, latent_grad = pl.pallas_call(
        fused,
        out_shape=[jax.ShapeDtypeStruct((HEADS_DEV, QK, TOK), bf16), jax.ShapeDtypeStruct((PIECE, QK), f32)],
        in_specs=[hbm] * 3 + [smem] * 2,
        out_specs=[hbm] * 2,
        scratch_shapes=[
            vmem((HEADS_DEV, QK, TOK), bf16),
            vmem((TOK, HEADS_DEV, LAT), bf16),
            vmem((WIDE, ROWS), bf16),
            vmem((ROWS, LAT), bf16),
            vmem((WIN, WIDE), bf16),
            vmem((WIDE, WIN), bf16),
            vmem((WIN, ROWS), f32),
            vmem((WIN, ROWS), f32),
            vmem((WIN, ROWS), bf16),
            vmem((WIN, ROWS), bf16),
            vmem((8, ROWS), f32),
            vmem((1, ROWS), i32),
            vmem((1, ROWS), i32),
            vmem((WIN, WIDE), f32),
            vmem(block_shape, bf16),
            vmem(block_shape, bf16),
            vmem(block_shape, bf16),
            vmem(block_shape, bf16),
            vmem(((BACK + 1) * HALF, WIDE), bf16),
            vmem(((BACK + 1) * HALF, WIDE), bf16),
            vmem((3, (BACK + 1) * PIECE, WIDE), bf16),
            vmem((3, (BACK + 1) * PIECE, WIDE), bf16),
            vmem((3, PIECE, WIDE), bf16),
            vmem((3, PIECE, WIDE), bf16),
            vmem((PIECE, WIDE), bf16),
            vmem((PIECE, WIDE), bf16),
            vmem((PIECE, QK), f32),
            dma((3,)), dma((6,)),
            dma, dma, dma((3,)), dma((3,)), dma((3, 3)), dma((3, 3)), dma((4,)), dma((4,)),
            dma((4, 2)), dma((4, 2)), dma((4, 2)), dma((4, 2)),
            dma, dma, dma((3,)), dma((3,)), dma((3,)), dma((3,)), dma, dma,
        ],
        compiler_params=pltpu.CompilerParams(
            collective_id=0, has_side_effects=True, vmem_limit_bytes=VMEM_BYTES
        ),
        cost_estimate=pl.CostEstimate(flops=8_000_000_000, bytes_accessed=8_000_000, transcendentals=1_300_000),
    )(jnp.transpose(queries, (1, 2, 0)), jnp.transpose(latent_kv), out_grad, lengths, block_plan)

    query_grad, latent_grad = pl.pallas_call(
        place,
        out_shape=[jax.ShapeDtypeStruct(query_grad.shape, bf16), jax.ShapeDtypeStruct(latent_grad.shape, f32)],
        in_specs=[hbm] * 2,
        out_specs=[hbm] * 2,
        scratch_shapes=[
            vmem(query_grad.shape, bf16), vmem(latent_grad.shape, f32), dma((HEADS_DEV + 1,)), dma((HEADS_DEV + 1,)),
        ],
        compiler_params=pltpu.CompilerParams(vmem_limit_bytes=VMEM_BYTES),
    )(query_grad, latent_grad)
    return jnp.transpose(query_grad, (2, 0, 1)), latent_grad


def solution(mesh):
    return jax.shard_map(
        on_device,
        mesh=mesh,
        in_specs=(P("ctx", "head", None), P("ctx", None), P("ctx", "head", None), P(), P()),
        out_specs=(P("ctx", "head", None), P(("ctx", "head"), None)),
        check_vma=False,
    )
```

```python
import functools

import jax
import jax.numpy as jnp
from jax import lax
from jax.experimental import pallas as pl
from jax.experimental.pallas import tpu as pltpu
from jax.sharding import PartitionSpec as P

BLOCK = 128
SCORE_SCALE = 192.0 ** (-0.5)
MASKED_FILL = -1e30
MESH = pl.DeviceIdType.MESH

HEADS_DEV = 4
TOK = 256
ROWS = TOK * HEADS_DEV
QK = 576
LAT = 512
WIDE = 640
BACK = 4
WIN = (BACK + 1) * TOK
CHUNK = 256
TILE = 128
STRIP = QK // 4
PIECE = 32
HALF = TOK // 2
FAR = 16
VMEM_BYTES = 63 * 1024 * 1024

NT = (((1,), (1,)), ((), ()))


def mm(a, b):
    return jnp.dot(a, b, preferred_element_type=jnp.float32)


def mm_nt(a, b):
    return lax.dot_general(a, b, NT, preferred_element_type=jnp.float32)


def fused(
    q_hbm, k_hbm, g_hbm, len_ref, plan_ref,
    dq_out, lat_out,
    q_in, g_in, q_all, g_all, win, win_t, scores, vgrads, probs, sgrads,
    top, start_of, pos_of, grads, dq0, dq1, mid, got,
    r1_out, r1_in, r2_out, r2_in, r3_out, r3_in, r4_out, r4_in, lat,
    in_sem, out_sem, s1, v1, sx, vx, s2, v2, s3, v3, st, vt, su, vu, sr1, vr1, sr2, vr2, sr3, vr3, sr4, vr4,
):
    ctx = lax.axis_index("ctx")
    head = lax.axis_index("head")
    n_ctx = lax.axis_size("ctx")
    n_y = 4
    y = head // 2
    core = head % 2
    x = ctx % 4
    zbase = ctx - x

    def at_ctx(by):
        return {"ctx": lax.rem(ctx + by + n_ctx, n_ctx)}

    def at_y(by):
        return {"head": lax.rem(y + by, n_y) * 2 + core}

    sibling = {"head": y * 2 + (1 - core)}

    peers = [at_ctx(b) for b in (1, 2, 3, 4, -1, -2, -3, -4, FAR, -FAR)]
    peers += [at_y(b) for b in (1, 2, 3)] + [sibling]
    own_at = BACK * TOK
    load_k = pltpu.make_async_copy(k_hbm, win_t.at[pl.ds(0, QK), pl.ds(own_at, TOK)], in_sem.at[0])
    load_q = pltpu.make_async_copy(q_hbm, q_in, in_sem.at[1])
    load_g = pltpu.make_async_copy(g_hbm, g_in, in_sem.at[2])
    load_k.start()
    load_q.start()
    load_g.start()
    barrier = pltpu.get_barrier_semaphore()
    for peer in peers:
        pl.semaphore_signal(barrier, inc=1, device_id=peer, device_id_type=MESH)
    win_t[QK:, :] = jnp.zeros((WIDE - QK, WIN), jnp.bfloat16)
    pl.semaphore_wait(barrier, len(peers))
    keys_of_core = pl.ds(pl.multiple_of(core * HALF, HALF), HALF)
    columns = pl.ds(pl.multiple_of(y * STRIP, 16), STRIP)

    def half(slot):
        return win_t.at[pl.ds(0, QK), pl.ds(pl.multiple_of(slot * TOK + core * HALF, HALF), HALF)]

    def piece(slot):
        return win_t.at[columns, pl.ds(pl.multiple_of(slot * TOK + core * HALF, HALF), HALF)]

    def remote(src, dst, ss, rs, to):
        return pltpu.make_async_remote_copy(
            src_ref=src, dst_ref=dst, send_sem=ss, recv_sem=rs, device_id=to, device_id_type=MESH
        )

    hops = (1, 3, 2)
    beside = {d: remote(k_hbm.at[columns, keys_of_core], piece(BACK - d), sx.at[d - 1], vx.at[d - 1], at_ctx(d)) for d in hops}
    for d in hops:
        beside[d].start()
    up = [remote(k_hbm.at[:, keys_of_core], half(0), s1, v1, at_ctx(BACK))]

    load_q.wait()
    q_all[QK:, :] = jnp.zeros((WIDE - QK, ROWS), jnp.bfloat16)
    for b in range(2):
        for h in range(HEADS_DEV):
            at = b * 512 + h * BLOCK
            q_all[:QK, at:at + BLOCK] = q_in[h, :, b * BLOCK:(b + 1) * BLOCK]

    lane = lax.broadcasted_iota(jnp.int32, (1, ROWS), 1)
    q_pos = ctx * TOK + (lane // 512) * BLOCK + lane % BLOCK
    begin = jnp.zeros((1, ROWS), jnp.int32)
    total = jnp.int32(0)
    for d in range(len_ref.shape[0]):
        begin = jnp.where(q_pos >= total, total, begin)
        total = total + len_ref[d]
    pos_of[...] = q_pos
    start_of[...] = begin
    top[...] = jnp.full(top.shape, MASKED_FILL, jnp.float32)

    def tile_scores(slot, lane0, count, width, turn=False):
        rows = pl.ds(pl.multiple_of(slot * TOK, TOK), TOK)
        if turn:
            keys = jnp.transpose(win_t[:, rows])
            win[rows, :] = keys
        else:
            keys = win[rows, :]
        row = lax.broadcasted_iota(jnp.int32, (TOK, width), 0)
        k_pos = (ctx - BACK + slot) * TOK + row

        def chunk(n, _):
            lanes = pl.ds(pl.multiple_of(lane0 + n * width, width), width)
            s = mm(keys, q_all[:, lanes]) * SCORE_SCALE
            allowed = (k_pos >= start_of[:, lanes]) & (k_pos <= pos_of[:, lanes])
            s = jnp.where(allowed, s, MASKED_FILL)
            scores[rows, lanes] = s
            top[:, lanes] = jnp.maximum(top[:, lanes], jnp.max(s.reshape(TOK // 8, 8, width), axis=0))
            vgrads[rows, lanes] = mm_nt(keys[:, :LAT], g_all[lanes, :])
            return 0

        if count == 1:
            chunk(0, 0)
        else:
            lax.fori_loop(0, count, chunk, 0)

    def earlier_scores(lane0, width):
        def step(slot, _):
            tile_scores(slot, lane0, 1, width)
            return 0

        lax.fori_loop(0, BACK, step, 0)

    second, third = {}, {}
    for d in hops:
        slot = BACK - d
        beside[d].wait_recv()
        second[d] = [
            remote(piece(slot), piece(slot), s2.at[d - 1, b - 1], v2.at[d - 1, b - 1], at_y(b)) for b in (1, 3, 2)
        ]
        for copy in second[d]:
            copy.start()
        if d == hops[0]:
            for copy in up:
                copy.start()

    load_g.wait()
    to_row = lax.broadcasted_iota(jnp.int32, (CHUNK, CHUNK), 0)
    from_row = lax.broadcasted_iota(jnp.int32, (CHUNK, CHUNK), 1)
    shuffle = (from_row == (to_row % 64) * HEADS_DEV + to_row // 64).astype(jnp.bfloat16)

    def shuffle_rows(k):
        rows = g_in[k * 64:(k + 1) * 64].reshape(CHUNK, LAT)
        rows = mm(shuffle, rows).astype(jnp.bfloat16)
        for h in range(HEADS_DEV):
            at = (k // 2) * 512 + h * BLOCK + (k % 2) * 64
            g_all[at:at + 64, :] = rows[h * 64:(h + 1) * 64, :]

    for k in range(4):
        shuffle_rows(k)
    load_k.wait()
    tile_scores(BACK, 512, 4, BLOCK, True)
    def exchange(slot):
        third[slot] = remote(half(slot), half(slot), s3.at[slot], v3.at[slot], sibling)
        third[slot].start()

    for d in hops:
        for copy in second[d]:
            copy.wait_recv()
        exchange(BACK - d)
        if d == hops[0]:
            for copy in up:
                copy.wait_recv()
            exchange(0)
    for slot in (BACK - hops[0], 0, BACK - hops[1], BACK - hops[2]):
        third[slot].wait_recv()
        tile_scores(slot, 512, 1, BLOCK, True)

    def query_chunk(lane0, width, out, h):
        lanes = slice(lane0, lane0 + width)
        tile = TILE * CHUNK // width
        leads = lane0 == ROWS // 2
        peak = jnp.max(top[:, lanes], axis=0, keepdims=True)

        def weigh(i, carry):
            denom, mix = carry
            rows = pl.ds(pl.multiple_of(i * tile, tile), tile)
            p = jnp.exp(scores[rows, lanes] - peak)
            scores[rows, lanes] = p
            pd = p * vgrads[rows, lanes]
            denom = denom + jnp.sum(p.reshape(tile // 8, 8, width), axis=0)
            mix = mix + jnp.sum(pd.reshape(tile // 8, 8, width), axis=0)
            return denom, mix

        zero = jnp.zeros((8, width), jnp.float32)
        denom, mix = lax.fori_loop(0, WIN // tile, weigh, (zero, zero), unroll=leads)
        inv = 1.0 / jnp.sum(denom, axis=0, keepdims=True)
        delta = jnp.sum(mix, axis=0, keepdims=True) * inv

        def finish(i, _):
            rows = pl.ds(pl.multiple_of(i * tile, tile), tile)
            p = scores[rows, lanes] * inv
            probs[rows, lanes] = p.astype(jnp.bfloat16)
            sgrads[rows, lanes] = (p * (vgrads[rows, lanes] - delta)).astype(jnp.bfloat16)
            return 0

        lax.fori_loop(0, WIN // tile, finish, 0, unroll=leads)
        grad = (mm(win_t[:QK, :], sgrads[:, lanes]) * SCORE_SCALE).astype(jnp.bfloat16)
        for k in range(width // BLOCK):
            out[h + k] = grad[:, k * BLOCK:(k + 1) * BLOCK]

    ways = ((slice(0, QK // 2), FAR), (slice(QK // 2, QK), -FAR))
    trade = []
    for k in range(HEADS_DEV):
        if k > 0:
            earlier_scores(512 + k * BLOCK, BLOCK)
        query_chunk(512 + k * BLOCK, BLOCK, dq1, k)
        for w, (rows, by) in enumerate(ways):
            copy = remote(dq1.at[k, rows], mid.at[k, rows], st.at[k, w], vt.at[k, w], at_ctx(by))
            copy.start()
            trade.append(copy)
    onward = []

    def pass_on(k):
        for w, (rows, by) in enumerate(ways):
            trade[2 * k + w].wait_recv()
            copy = remote(mid.at[k, rows], got.at[k, rows], su.at[k, w], vu.at[k, w], at_ctx(by))
            copy.start()
            onward.append(copy)

    for n in range(2):
        tile_scores(BACK, n * CHUNK, 1, CHUNK)
        earlier_scores(n * CHUNK, CHUNK)
        query_chunk(n * CHUNK, CHUNK, dq0, 2 * n)
    keep = [pltpu.make_async_copy(dq0, dq_out.at[:, :, :BLOCK], out_sem.at[0])]
    keep[0].start()

    def owned(slot, of_y, of_core):
        return pl.ds(pl.multiple_of(slot * TOK + of_y * 2 * PIECE + of_core * PIECE, PIECE), PIECE)

    def key_grads(slot, _):
        rows = pl.ds(pl.multiple_of(slot * TOK, TOK), TOK)
        grads[rows, :] = mm_nt(sgrads[rows, :], q_all[...]) * SCORE_SCALE
        grads[rows, :LAT] += mm(probs[rows, :], g_all[...])
        for yy in range(n_y):
            held = pl.ds(pl.multiple_of(slot * HALF + yy * PIECE, PIECE), PIECE)
            r1_out[held, :] = grads[owned(slot, yy, 1 - core), :].astype(jnp.bfloat16)
        return 0

    lax.fori_loop(0, BACK + 1, key_grads, 0)
    swap = remote(r1_out, r1_in, sr1, vr1, sibling)
    swap.start()
    swap.wait_recv()

    def join(slot, _):
        for yy in range(n_y):
            held = pl.ds(pl.multiple_of(slot * HALF + yy * PIECE, PIECE), PIECE)
            grads[owned(slot, yy, core), :] += r1_in[held, :].astype(jnp.float32)
        return 0

    lax.fori_loop(0, BACK + 1, join, 0)
    spread = []
    for b in (1, 3, 2):
        to = lax.rem(y + b, n_y)
        for slot in range(BACK + 1):
            r2_out[b - 1, slot * PIECE:(slot + 1) * PIECE, :] = grads[owned(slot, to, core), :].astype(jnp.bfloat16)
        copy = remote(r2_out.at[b - 1], r2_in.at[b - 1], sr2.at[b - 1], vr2.at[b - 1], at_y(b))
        copy.start()
        spread.append(copy)
    pass_on(0)
    pass_on(1)
    for copy in spread:
        copy.wait_recv()
    sums = []
    for slot in range(BACK + 1):
        part = grads[owned(slot, y, core), :]
        for b in range(3):
            part = part + r2_in[b, slot * PIECE:(slot + 1) * PIECE, :].astype(jnp.float32)
        sums.append(part)

    along = []
    for d in (1, 3, 2):
        r3_out[d - 1] = sums[BACK - d].astype(jnp.bfloat16)
        to = {"ctx": zbase + lax.rem(x - d + 4, 4)}
        copy = remote(r3_out.at[d - 1], r3_in.at[d - 1], sr3.at[d - 1], vr3.at[d - 1], to)
        copy.start()
        along.append(copy)
    pass_on(2)
    for copy in along:
        copy.wait_recv()
    here = sums[BACK]
    before = sums[0]
    for d in (1, 2, 3):
        part = r3_in[d - 1].astype(jnp.float32)
        inside = x + d < 4
        here = here + jnp.where(inside, part, 0.0)
        before = before + jnp.where(inside, 0.0, part)
    r4_out[...] = before.astype(jnp.bfloat16)
    down = remote(r4_out, r4_in, sr4, vr4, at_ctx(-4))
    down.start()
    pass_on(3)
    down.wait_recv()
    lat[...] = (here + r4_in[...].astype(jnp.float32))[:, :QK]
    keep.append(pltpu.make_async_copy(lat, lat_out, out_sem.at[1]))
    keep[1].start()
    sent = up + [c for d in hops for c in second[d] + [beside[d]]] + [third[slot] for slot in range(BACK)]
    for copy in sent + [swap] + spread + along + [down] + trade:
        copy.wait_send()
    traded = plan_ref[2 * ctx + 1] != ctx
    for k in range(HEADS_DEV):
        for copy in onward[2 * k:2 * k + 2]:
            copy.wait_recv()
        dq1[k] = jnp.where(traded, got[k], dq1[k])
        keep.append(pltpu.make_async_copy(dq1.at[k], dq_out.at[k, :, BLOCK:], out_sem.at[2 + k]))
        keep[-1].start()
    for copy in onward:
        copy.wait_send()
    for copy in keep:
        copy.wait()


def place(dq_in, lat_in, dq_out, lat_out, dq_held, lat_held, in_sem, out_sem):
    parts = [(dq_in.at[h], dq_held.at[h], dq_out.at[h]) for h in range(HEADS_DEV)] + [(lat_in, lat_held, lat_out)]
    loads = [pltpu.make_async_copy(src, held, in_sem.at[i]) for i, (src, held, _) in enumerate(parts)]
    stores = [pltpu.make_async_copy(held, dst, out_sem.at[i]) for i, (_, held, dst) in enumerate(parts)]
    for load in loads:
        load.start()
    for load, store in zip(loads, stores):
        load.wait()
        store.start()
    for store in stores:
        store.wait()


def on_device(queries, latent_kv, out_grad, lengths, block_plan):
    bf16, f32, i32 = jnp.bfloat16, jnp.float32, jnp.int32
    hbm = pl.BlockSpec(memory_space=pl.ANY)
    smem = pl.BlockSpec(memory_space=pltpu.SMEM)
    dma = pltpu.SemaphoreType.DMA
    block_shape = (HEADS_DEV, QK, BLOCK)
    vmem = pltpu.VMEM
    query_grad, latent_grad = pl.pallas_call(
        fused,
        out_shape=[jax.ShapeDtypeStruct((HEADS_DEV, QK, TOK), bf16), jax.ShapeDtypeStruct((PIECE, QK), f32)],
        in_specs=[hbm] * 3 + [smem] * 2,
        out_specs=[hbm] * 2,
        scratch_shapes=[
            vmem((HEADS_DEV, QK, TOK), bf16),
            vmem((TOK, HEADS_DEV, LAT), bf16),
            vmem((WIDE, ROWS), bf16),
            vmem((ROWS, LAT), bf16),
            vmem((WIN, WIDE), bf16),
            vmem((WIDE, WIN), bf16),
            vmem((WIN, ROWS), f32),
            vmem((WIN, ROWS), f32),
            vmem((WIN, ROWS), bf16),
            vmem((WIN, ROWS), bf16),
            vmem((8, ROWS), f32),
            vmem((1, ROWS), i32),
            vmem((1, ROWS), i32),
            vmem((WIN, WIDE), f32),
            vmem(block_shape, bf16),
            vmem(block_shape, bf16),
            vmem(block_shape, bf16),
            vmem(block_shape, bf16),
            vmem(((BACK + 1) * HALF, WIDE), bf16),
            vmem(((BACK + 1) * HALF, WIDE), bf16),
            vmem((3, (BACK + 1) * PIECE, WIDE), bf16),
            vmem((3, (BACK + 1) * PIECE, WIDE), bf16),
            vmem((3, PIECE, WIDE), bf16),
            vmem((3, PIECE, WIDE), bf16),
            vmem((PIECE, WIDE), bf16),
            vmem((PIECE, WIDE), bf16),
            vmem((PIECE, QK), f32),
            dma((3,)), dma((6,)),
            dma, dma, dma((3,)), dma((3,)), dma((3, 3)), dma((3, 3)), dma((4,)), dma((4,)),
            dma((4, 2)), dma((4, 2)), dma((4, 2)), dma((4, 2)),
            dma, dma, dma((3,)), dma((3,)), dma((3,)), dma((3,)), dma, dma,
        ],
        compiler_params=pltpu.CompilerParams(
            collective_id=0, has_side_effects=True, vmem_limit_bytes=VMEM_BYTES
        ),
        cost_estimate=pl.CostEstimate(flops=8_000_000_000, bytes_accessed=8_000_000, transcendentals=1_300_000),
    )(jnp.transpose(queries, (1, 2, 0)), jnp.transpose(latent_kv), out_grad, lengths, block_plan)

    query_grad, latent_grad = pl.pallas_call(
        place,
        out_shape=[jax.ShapeDtypeStruct(query_grad.shape, bf16), jax.ShapeDtypeStruct(latent_grad.shape, f32)],
        in_specs=[hbm] * 2,
        out_specs=[hbm] * 2,
        scratch_shapes=[
            vmem(query_grad.shape, bf16), vmem(latent_grad.shape, f32), dma((HEADS_DEV + 1,)), dma((HEADS_DEV + 1,)),
        ],
        compiler_params=pltpu.CompilerParams(vmem_limit_bytes=VMEM_BYTES),
    )(query_grad, latent_grad)
    return jnp.transpose(query_grad, (2, 0, 1)), latent_grad


def solution(mesh):
    return jax.shard_map(
        on_device,
        mesh=mesh,
        in_specs=(P("ctx", "head", None), P("ctx", None), P("ctx", "head", None), P(), P()),
        out_specs=(P("ctx", "head", None), P(("ctx", "head"), None)),
        check_vma=False,
    )
```
